32 devices in a mesh: seq: 4 (over z), head: 4 (over y, x), dp: 2 (over core).
Axes of the slice: x: 2, y: 2, z: 4, core: 2. Of those that a mesh axis runs over, the one named last changes fastest.
Arguments:
- x_in: bfloat16 [2048, 8192], P(('dp', 'seq'), 'head'), parts along dimension 0, as said below
- bc_in: bfloat16 [2048, 2048], P(('dp', 'seq'), 'head'), parts along dimension 0, may hold values from -6 to 6
- z_in: bfloat16 [2048, 8192], P(('dp', 'seq'), 'head'), parts along dimension 0, may hold values from -6 to 6
- dt_raw: float32 [2048, 128], P(('dp', 'seq'), 'head'), parts along dimension 0, as said below
- dt_bias: float32 [128], P('head'), as said below
- a_log: float32 [128], P('head'), as said below
- d_skip: float32 [128], P('head'), may hold values from 0.5 to 1.5
- conv_x: float32 [4, 8192], P(None, 'head'), may hold values from -3 to 3
- conv_bc: float32 [4, 2048], P(None, 'head'), may hold values from -3 to 3
- norm_gain: float32 [8192], P('head'), may hold values from 0.1 to 1.9
- out_weight: bfloat16 [8192, 4096], P('head', 'seq'), may hold values from -0.09375 to 0.09375
Outputs:
- layer_out: bfloat16 [2048, 4096], P(('dp', 'seq'), 'head'), parts along dimension 0
The draws below stay inside these ranges and needn't reach their ends.
There are 2 independent parts, one for each index of `dp`. The reference program is written for one: setup_inputs(seed, part) draws one part's arguments, and reference() takes and returns one part's arrays. A program takes and returns all parts, laid end to end along the dimension named above; an argument that names none is the same for every part. Nothing has to cross between parts.
Inputs may be any that keep to these rules, and one draw needn't show every extreme that they name: `x_in`: finite values. `dt_raw`: finite values. `dt_bias`: finite values. `a_log`: finite values.
All inputs are finite; a program needn't handle non-finite values.
Results may differ from the reference program's by a relative error of at most 0.0051.
Values may be sent and summed in bfloat16 or wider, within the bound.
A program may use at most 192 MiB of HBM per device.

```python
import math
import jax
import jax.numpy as jnp
from jax import lax

D = 4096
H = 128
P_SIZE = 64
N = 128
G = 8
BLOCK = 256
CONV = 4
LETTERS_PER_PART = 256
DI = 8192
LETTER_TOTAL = 1024


def head_rates(key):
    folded = jax.random.fold_in(key, 11)
    pick_key, slow_key, fast_key = jax.random.split(folded, 3)
    spread_key = jax.random.fold_in(key, 13)
    slow_heads = jax.random.uniform(pick_key, (H,)) < 0.5
    slow_rate = jax.random.uniform(slow_key, (H,), jnp.float32, 0.3, 0.75)
    fast_rate = jax.random.uniform(fast_key, (H,), jnp.float32, 0.7, 1.4)
    head_factor = jnp.exp(jax.random.uniform(spread_key, (H,), jnp.float32, -0.7, 0.7))
    window = max(BLOCK // 6, 2)
    slow_step = 2.0 / math.sqrt(LETTER_TOTAL * N)
    fast_step = 2.0 / math.sqrt(window * N)
    step_base = jnp.where(slow_heads, slow_step, fast_step) * head_factor
    decay_rate = jnp.where(slow_heads, slow_rate / LETTER_TOTAL, fast_rate / window) / step_base
    return (step_base, decay_rate)


def spike_markers(key):
    spots = jax.random.randint(jax.random.fold_in(key, 23), (2,), CONV, LETTER_TOTAL)
    places = jnp.arange(LETTER_TOTAL, dtype=jnp.int32)
    agreement_tally = jnp.any(places[:, None] == spots[None, :], axis=1)
    adjacent_lines = jnp.any((places[:, None] >= spots[None, :] - (CONV - 1)) & (places[:, None] <= spots[None, :]), axis=1)
    return (agreement_tally, adjacent_lines)


def draw_a_log(key, part):
    step_base, decay_rate = head_rates(key)
    return jnp.log(decay_rate).astype(jnp.float32)


def draw_dt_bias(key, part):
    step_base, decay_rate = head_rates(key)
    return jnp.log(jnp.expm1(step_base)).astype(jnp.float32)


def draw_dt_raw(key, part):
    agreement_tally, adjacent_lines = spike_markers(key)
    noise_key, level_key = jax.random.split(jax.random.fold_in(key, 5))
    noise = 0.5 * jnp.clip(jax.random.normal(noise_key, (LETTER_TOTAL, H), jnp.float32), -4.0, 4.0)
    levels = jax.random.uniform(level_key, (LETTER_TOTAL // LETTERS_PER_PART, 1), jnp.float32, -0.7, 0.7)
    levels = jnp.repeat(levels, LETTERS_PER_PART, axis=0)
    jump = jnp.where(agreement_tally, math.log(0.8 * LETTER_TOTAL), 0.0)[:, None]
    return (noise + levels + jump).astype(jnp.float32)


def draw_x_in(key, part):
    agreement_tally, adjacent_lines = spike_markers(key)
    value_key = jax.random.fold_in(jax.random.fold_in(key, 7), 0)
    values = jax.random.normal(value_key, (LETTER_TOTAL, H * P_SIZE), jnp.float32)
    values = values * jnp.where(adjacent_lines, 0.001, 1.0)[:, None]
    return values.astype(jnp.bfloat16)


def with_spikes(entries, rng, source, target, blocks, factor):
    owner, partner = [(jnp.arange(entries.shape[position]) // (entries.shape[position] // blocks)).reshape([-1 if axis == position else 1 for axis in range(entries.ndim)]) for position in (source, target)]
    chosen = jax.random.permutation(rng, blocks)[partner]
    strong = (owner == chosen) | (owner == (partner + blocks // 2) % blocks)
    return jnp.where(strong, factor * entries, entries)


def level_of(stream_key, shape, cuts, least, largest):
    factor_of, own = 1.0, jax.random.fold_in(stream_key, 6)
    for axis_at, shards_of in cuts:
        steps = jnp.exp(jax.random.uniform(jax.random.fold_in(own, axis_at), (shards_of,), jnp.float32, least / len(cuts), largest / len(cuts)))
        factor_of = factor_of * jnp.repeat(steps, shape[axis_at] // shards_of).reshape([-1 if axis == axis_at else 1 for axis in range(len(shape))])
    return factor_of


def gaussian(key, extent, width, limit, cuts=(), kind=jnp.bfloat16):
    array = width * jax.random.normal(key, extent, jnp.float32)
    if cuts:
        array = array * level_of(key, extent, cuts, -0.22, 0.18)
    return jnp.clip(array, -limit, limit).astype(kind)


def gaussian_with(rng, dims, scale, limit, pieces, heavy, held_as=jnp.bfloat16):
    result = scale * jax.random.normal(rng, dims, jnp.float32)
    if pieces:
        result = result * level_of(rng, dims, pieces, -0.22, 0.18)
    return jnp.clip(with_spikes(result, jax.random.fold_in(rng, 3), *heavy), -limit, limit).astype(held_as)


def setup_inputs(seed: int = 0, part: int = 0) -> dict:
    keys = jax.random.split(jax.random.key(seed), 12)
    part_splits = jax.random.split(jax.random.fold_in(keys[11], part), 12)
    x_in = draw_x_in(jax.random.fold_in(jax.random.fold_in(keys[11], part), 71), part)
    bc_in = gaussian(part_splits[1], (LETTER_TOTAL, G * 2 * N), 1.0, 6.0, ((0, 4), (1, 4)))
    z_in = gaussian(part_splits[2], (LETTER_TOTAL, DI), 1.0, 6.0, ((0, 4), (1, 4)))
    dt_raw = draw_dt_raw(jax.random.fold_in(jax.random.fold_in(keys[11], part), 71), part)
    dt_bias = draw_dt_bias(jax.random.fold_in(keys[11], 71), part)
    a_log = draw_a_log(jax.random.fold_in(keys[11], 71), part)
    d_skip = jnp.clip(0.5 + 1.0 * jax.random.uniform(keys[6], (H,), jnp.float32) ** level_of(keys[6], (H,), ((0, 4),), -0.2, 0.2), 0.5, 1.5)
    conv_x = gaussian(keys[7], (CONV, DI), 0.5, 3.0, ((1, 4),), jnp.float32)
    conv_bc = gaussian(keys[8], (CONV, G * 2 * N), 0.5, 3.0, ((1, 4),), jnp.float32)
    norm_gain = jnp.clip(1.0 + 0.18 * jax.random.normal(keys[9], (DI,), jnp.float32), 0.1, 1.9)
    out_weight = gaussian_with(keys[10], (DI, D), DI ** -0.5, 0.09375, ((0, 4), (1, 4)), (0, 1, 4, 2.0))
    return dict(x_in=x_in, bc_in=bc_in, z_in=z_in, dt_raw=dt_raw, dt_bias=dt_bias, a_log=a_log, d_skip=d_skip, conv_x=conv_x, conv_bc=conv_bc, norm_gain=norm_gain, out_weight=out_weight)


epsilon = 1e-05

def causal_conv(values, weight):
    length = values.shape[0]
    padded = jnp.concatenate([jnp.zeros((CONV - 1, values.shape[1]), jnp.float32), values], axis=0)
    summed = jnp.zeros(values.shape, jnp.float32)
    for offset in range(CONV):
        summed = summed + weight[offset][None, :] * padded[offset:offset + length]
    return summed

def reference(x_in, bc_in, z_in, dt_raw, dt_bias, a_log, d_skip, conv_x, conv_bc, norm_gain, out_weight):
    input_convolved = jax.nn.silu(causal_conv(x_in.astype(jnp.float32), conv_x)).astype(jnp.bfloat16)
    bc_conv = jax.nn.silu(causal_conv(bc_in.astype(jnp.float32), conv_bc)).astype(jnp.bfloat16)
    step_sizes = jax.nn.softplus(dt_raw + dt_bias[None, :])
    log_decay = -jnp.exp(a_log)[None, :] * step_sizes
    blocks = LETTER_TOTAL // BLOCK
    per_group = H // G
    bc_groups = bc_conv.reshape(LETTER_TOTAL, G, 2, N)
    b_mat = bc_groups[:, :, 0]
    c_mat = bc_groups[:, :, 1]
    x_blocks = input_convolved.reshape(blocks, BLOCK, H, P_SIZE)
    b_blocks = b_mat.reshape(blocks, BLOCK, G, N)
    c_blocks = c_mat.reshape(blocks, BLOCK, G, N)
    decay_blocks = log_decay.reshape(blocks, BLOCK, H)
    step_blocks = step_sizes.reshape(blocks, BLOCK, H)
    places = jnp.arange(BLOCK, dtype=jnp.int32)
    lower = places[:, None] >= places[None, :]

    def advance(state, input_rows):
        x_here, b_here, c_here, decay_here, step_here = input_rows
        running = jnp.cumsum(decay_here, axis=0)
        scores = jnp.einsum('ign,jgn->gij', c_here.astype(jnp.float32), b_here.astype(jnp.float32))
        score_heads = jnp.repeat(scores, per_group, axis=0)
        running_heads = running.T
        spread = running_heads[:, :, None] - running_heads[:, None, :]
        spread = jnp.where(lower[None], spread, -jnp.inf)
        mixing = (score_heads * jnp.exp(spread) * step_here.T[:, None, :]).astype(jnp.bfloat16)
        within = jnp.einsum('hij,jhp->ihp', mixing.astype(jnp.float32), x_here.astype(jnp.float32))
        until_finish = jnp.exp(running[-1][None, :] - running) * step_here
        b_heads = jnp.repeat(b_here.astype(jnp.float32), per_group, axis=1)
        weighted_b = (b_heads * until_finish[:, :, None]).astype(jnp.bfloat16)
        fresh = jnp.einsum('jhn,jhp->hnp', weighted_b.astype(jnp.float32), x_here.astype(jnp.float32))
        since_beginning = jnp.repeat(c_here.astype(jnp.float32), per_group, axis=1) * jnp.exp(running)[:, :, None]
        across = jnp.einsum('ihn,hnp->ihp', since_beginning, state, precision=lax.Precision.HIGHEST)
        mixed = within + across + d_skip[None, :, None] * x_here.astype(jnp.float32)
        state = jnp.exp(running[-1])[:, None, None] * state + fresh
        return (state, mixed.reshape(BLOCK, H * P_SIZE))
    start_state = jnp.zeros((H, N, P_SIZE), jnp.float32)
    unused, outputs = lax.scan(advance, start_state, (x_blocks, b_blocks, c_blocks, decay_blocks, step_blocks))
    mixed = outputs.reshape(LETTER_TOTAL, H * P_SIZE)
    gated = mixed * jax.nn.silu(z_in.astype(jnp.float32))
    mean_square = lax.optimization_barrier(jnp.mean(gated * gated, axis=1, keepdims=True))
    normed = (gated * lax.rsqrt(mean_square + epsilon) * norm_gain[None, :]).astype(jnp.bfloat16)
    layer_out = jnp.dot(normed, out_weight, preferred_element_type=jnp.float32)
    return layer_out.astype(jnp.bfloat16)
```

```python
import jax
import jax.numpy as jnp
from jax import lax
from jax.experimental import pallas as pl
from jax.experimental.pallas import tpu as pltpu
from jax.sharding import PartitionSpec as P

H = 128
P_SIZE = 64
N = 128
BLOCK = 256
CONV = 4
CHUNK_HEADS = 4
TAIL = 16
MESH = pl.DeviceIdType.MESH


epsilon = 1e-05


def silu(v):
    return v / (1.0 + jnp.exp(-v))


def conv_silu(joined, tail, current, weight):
    height = current.shape[0]
    joined[:TAIL] = tail.astype(jnp.float32)
    joined[TAIL:] = current.astype(jnp.float32)
    summed = weight[0:1] * joined[pl.ds(TAIL - CONV + 1, height)]
    for offset in range(1, CONV):
        summed = summed + weight[offset : offset + 1] * joined[
            pl.ds(TAIL - CONV + 1 + offset, height)
        ]
    return silu(summed).astype(jnp.bfloat16)


def own_block_kernel(
    per_group_chunks, x_ref, xt_ref, bc_ref, bct_ref, z_ref, cx_ref, cbc_ref, cols_ref, rows_ref,
    d_ref, p_ref, q_ref, fresh_ref, c_ref, joined, scores, b_turned,
):
    height, width = x_ref.shape

    @pl.when(lax.rem(pl.program_id(0), per_group_chunks) == 0)
    def _():
        bc = conv_silu(joined, bct_ref[...], bc_ref[...], cbc_ref[...])
        b_mat, c_mat = bc[:, :N], bc[:, N:]
        c_ref[...] = c_mat
        b_turned[...] = b_mat.astype(jnp.float32).T.astype(jnp.bfloat16)
        scores[...] = lax.dot_general(
            c_mat, b_mat, (((1,), (1,)), ((), ())), preferred_element_type=jnp.float32
        )

    x = conv_silu(joined, xt_ref[...], x_ref[...], cx_ref[...])
    x_wide = x.astype(jnp.float32)
    head_of = lax.broadcasted_iota(jnp.int32, (height, width), 1) // P_SIZE
    lower = lax.broadcasted_iota(jnp.int32, (height, height), 0) >= lax.broadcasted_iota(
        jnp.int32, (height, height), 1
    )
    cols = cols_ref[0]
    rows = rows_ref[0]
    within = d_ref[...] * x_wide
    until = jnp.zeros((height, width), jnp.float32)
    since = jnp.zeros((height, width), jnp.float32)
    for k in range(CHUNK_HEADS):
        spread = jnp.where(lower, cols[:, k : k + 1] - rows[k : k + 1], -jnp.inf)
        mixing = scores[...] * jnp.exp(spread) * rows[CHUNK_HEADS + k : CHUNK_HEADS + k + 1]
        mine = head_of == k
        within = within + jnp.dot(
            mixing.astype(jnp.bfloat16),
            jnp.where(mine, x_wide, 0.0).astype(jnp.bfloat16),
            preferred_element_type=jnp.float32,
        )
        until = jnp.where(mine, cols[:, CHUNK_HEADS + k : CHUNK_HEADS + k + 1], until)
        since = jnp.where(mine, cols[:, 2 * CHUNK_HEADS + k : 2 * CHUNK_HEADS + k + 1], since)
    gate = silu(z_ref[...].astype(jnp.float32))
    p_ref[...] = within * gate
    q_ref[...] = since * gate
    fresh_ref[...] = jnp.dot(
        b_turned[...], (x_wide * until).astype(jnp.bfloat16), preferred_element_type=jnp.float32
    )


def joined_kernel(
    size, parts, channels, p_ref, q_ref, fresh_ref, decay_ref, c_ref, gain_ref, w_ref, out_ref,
    state_in, state_out, gated, sums_out, sums_in, normed, partial, own, arrived, final,
    st_send, st_recv, ss_send, ss_recv, up_send, up_recv, dn_send, dn_recv,
    rs_send, rs_recv, pm_send, pm_recv,
):
    s = lax.axis_index("seq")
    h = lax.axis_index("head")
    height, width = p_ref.shape
    columns = w_ref.shape[1]
    rows = height // parts
    last = size - 1

    def copy(src, dst, send, recv, **where):
        return pltpu.make_async_remote_copy(
            src_ref=src, dst_ref=dst, send_sem=send, recv_sem=recv,
            device_id=where, device_id_type=MESH,
        )

    barrier = pltpu.get_barrier_semaphore()

    def greet(**where):
        pl.semaphore_signal(barrier, inc=1, device_id=where, device_id_type=MESH)

    @pl.when(s > 0)
    def _():
        greet(seq=s - 1)

    @pl.when(s < last)
    def _():
        greet(seq=s + 1)

    for k in range(1, size):
        greet(head=lax.rem(h + k, size))

    @pl.when(s != h)
    def _():
        greet(seq=h, head=s)

    one = jnp.int32(1)
    peers = (
        (size - 1) * one + jnp.where(s > 0, one, 0) + jnp.where(s < last, one, 0)
        + jnp.where(s != h, one, 0)
    )
    pl.semaphore_wait(barrier, peers)

    chunks = st_send.shape[0]
    wide = width // chunks
    groups = c_ref.shape[1] // N
    group_width = width // groups

    def state_copy(j):
        return copy(state_out.at[j], state_in.at[j], st_send.at[j], st_recv.at[j], seq=s + 1)

    @pl.when(s == 0)
    def _():
        state_in[...] = jnp.zeros_like(state_in)

    squares = jnp.zeros((height, 128), jnp.float32)
    for j in range(chunks):
        span = slice(j * wide, (j + 1) * wide)

        @pl.when(s > 0)
        def _():
            state_copy(j).wait_recv()

        @pl.when(s < last)
        def _():
            state_out[j] = (
                fresh_ref[:, span] + decay_ref[:, span] * state_in[j].astype(jnp.float32)
            ).astype(jnp.bfloat16)
            state_copy(j).start()

    for j in range(chunks):
        span = slice(j * wide, (j + 1) * wide)
        g = j * wide // group_width
        across = jnp.dot(
            c_ref[:, g * N : (g + 1) * N], state_in[j], preferred_element_type=jnp.float32
        )
        value = p_ref[:, span] + q_ref[:, span] * across
        gated[:, span] = value
        value = value * value
        for k in range(wide // 128):
            squares = squares + value[:, k * 128 : (k + 1) * 128]

    sums_out[...] = jnp.broadcast_to(jnp.sum(squares.T, axis=0, keepdims=True), sums_out.shape)

    def sums_copy(k):
        return copy(
            sums_out, sums_in.at[k - 1], ss_send.at[k - 1], ss_recv.at[k - 1],
            head=lax.rem(h + k, size),
        )

    for k in range(1, size):
        sums_copy(k).start()
    total = sums_out[...]
    for k in range(1, size):
        sums_copy(k).wait_recv()
        total = total + sums_in[k - 1]
    scale = lax.rsqrt(total / channels + epsilon)
    scale = jnp.broadcast_to(scale[0:1], (128, height)).T

    def up_copy(d, r):
        place = normed.at[s - d, pl.ds(r * rows, rows)]
        return copy(place, place, up_send.at[d, r], up_recv.at[d, r], seq=s + 1)

    def up_landed(d, r):
        place = normed.at[s - d, pl.ds(r * rows, rows)]
        return copy(place, place, up_send.at[d - 1, r], up_recv.at[d - 1, r], seq=s + 1)

    def down_copy(d, r):
        place = normed.at[s + d, pl.ds(r * rows, rows)]
        return copy(place, place, dn_send.at[d, r], dn_recv.at[d, r], seq=s - 1)

    def down_landed(d, r):
        place = normed.at[s + d, pl.ds(r * rows, rows)]
        return copy(place, place, dn_send.at[d - 1, r], dn_recv.at[d - 1, r], seq=s - 1)

    def partial_copy(t, r):
        slot = lax.rem(h - t + size, size) - 1
        return copy(
            partial.at[t, r], arrived.at[slot, r], rs_send.at[t, r], rs_recv.at[slot, r], head=t
        )

    def multiply(t, r):
        @pl.loop(0, columns // 256)
        def _(n):
            span = pl.ds(pl.multiple_of(n * 256, 256), 256)
            value = jnp.dot(
                normed[t, r * rows : (r + 1) * rows, :], w_ref[:, span],
                preferred_element_type=jnp.float32,
            )
            partial[t, r, :, span] = value.astype(jnp.bfloat16)

            @pl.when(h == t)
            def _():
                own[r, :, span] = value

        @pl.when(h != t)
        def _():
            partial_copy(t, r).start()

    for r in range(parts):
        some = slice(r * rows, (r + 1) * rows)
        for k in range(width // 128):
            span = slice(k * 128, (k + 1) * 128)
            normed[s, some, span] = (
                gated[some, span] * scale[some] * gain_ref[:, span]
            ).astype(jnp.bfloat16)

        @pl.when(s < last)
        def _():
            up_copy(0, r).start()

        @pl.when(s > 0)
        def _():
            down_copy(0, r).start()

    for r in range(parts):
        multiply(s, r)

    for d in range(1, size):
        for r in range(parts):
            @pl.when(s - d >= 0)
            def _():
                up_landed(d, r).wait_recv()
                if d < last:
                    @pl.when(s < last)
                    def _():
                        up_copy(d, r).start()

            @pl.when(s + d <= last)
            def _():
                down_landed(d, r).wait_recv()
                if d < last:
                    @pl.when(s > 0)
                    def _():
                        down_copy(d, r).start()

            @pl.when(s - d >= 0)
            def _():
                multiply(s - d, r)

            @pl.when(s + d <= last)
            def _():
                multiply(s + d, r)

    def final_copy(r):
        return copy(
            final.at[r], out_ref.at[pl.ds(r * rows, rows)], pm_send.at[r], pm_recv.at[r],
            seq=h, head=s,
        )

    for r in range(parts):
        value = own[r]
        for k in range(1, size):
            copy(
                partial.at[0, r], arrived.at[k - 1, r], rs_send.at[0, r], rs_recv.at[k - 1, r],
                head=lax.rem(h + k, size),
            ).wait_recv()
            value = value + arrived[k - 1, r].astype(jnp.float32)
        final[r] = value.astype(jnp.bfloat16)

        @pl.when(s != h)
        def _():
            final_copy(r).start()

        @pl.when(s == h)
        def _():
            out_ref[r * rows : (r + 1) * rows] = final[r]

    for r in range(parts):
        @pl.when(s != h)
        def _():
            final_copy(r).wait()

    for j in range(chunks):
        @pl.when(s < last)
        def _():
            state_copy(j).wait_send()

    for k in range(1, size):
        sums_copy(k).wait_send()

    for r in range(parts):
        for t in range(size):
            @pl.when(h != t)
            def _():
                partial_copy(t, r).wait_send()

        for d in range(last):
            @pl.when((s < last) & (s - d >= 0))
            def _():
                up_copy(d, r).wait_send()

            @pl.when((s > 0) & (s + d <= last))
            def _():
                down_copy(d, r).wait_send()


def square_shards(
    x_in, bc_in, z_in, dt_raw, dt_bias, a_log, d_skip, conv_x, conv_bc, norm_gain, out_weight
):
    size = lax.axis_size("seq")
    height, width = x_in.shape
    heads = dt_raw.shape[1]
    groups = bc_in.shape[1] // (2 * N)
    chunks = heads // CHUNK_HEADS
    per_group_chunks = chunks // groups
    wide = CHUNK_HEADS * P_SIZE
    tails = from_behind(
        jnp.concatenate([x_in[height - TAIL :], bc_in[height - TAIL :]], axis=1), "seq", 1
    )
    step_sizes = jax.nn.softplus(dt_raw + dt_bias[None, :])
    running = jnp.cumsum(-jnp.exp(a_log)[None, :] * step_sizes, axis=0)
    until_finish = jnp.exp(running[-1:] - running) * step_sizes
    cols = jnp.stack([running, until_finish, jnp.exp(running)])
    cols = cols.reshape(3, height, chunks, CHUNK_HEADS).transpose(2, 1, 0, 3)
    cols = cols.reshape(chunks, height, 3 * CHUNK_HEADS)
    rows = jnp.stack([running, step_sizes]).reshape(2, height, chunks, CHUNK_HEADS)
    rows = rows.transpose(2, 0, 3, 1).reshape(chunks, 2 * CHUNK_HEADS, height)
    decay = jnp.repeat(jnp.exp(running[-1]), P_SIZE)[None, :]
    skip = jnp.repeat(d_skip, P_SIZE)[None, :]

    first_bc = width // (2 * N)
    p, q, fresh, c_mat = pl.pallas_call(
        lambda *refs: own_block_kernel(per_group_chunks, *refs),
        grid=(chunks,),
        out_shape=(
            jax.ShapeDtypeStruct((height, width), jnp.float32),
            jax.ShapeDtypeStruct((height, width), jnp.float32),
            jax.ShapeDtypeStruct((N, width), jnp.float32),
            jax.ShapeDtypeStruct((height, groups * N), jnp.bfloat16),
        ),
        in_specs=[
            pl.BlockSpec((height, wide), lambda j: (0, j)),
            pl.BlockSpec((TAIL, wide), lambda j: (0, j)),
            pl.BlockSpec((height, 2 * N), lambda j: (0, j // per_group_chunks)),
            pl.BlockSpec((TAIL, 2 * N), lambda j: (0, first_bc + j // per_group_chunks)),
            pl.BlockSpec((height, wide), lambda j: (0, j)),
            pl.BlockSpec((CONV, wide), lambda j: (0, j)),
            pl.BlockSpec((CONV, 2 * N), lambda j: (0, j // per_group_chunks)),
            pl.BlockSpec((1, height, 3 * CHUNK_HEADS), lambda j: (j, 0, 0)),
            pl.BlockSpec((1, 2 * CHUNK_HEADS, height), lambda j: (j, 0, 0)),
            pl.BlockSpec((1, wide), lambda j: (0, j)),
        ],
        out_specs=(
            pl.BlockSpec((height, wide), lambda j: (0, j)),
            pl.BlockSpec((height, wide), lambda j: (0, j)),
            pl.BlockSpec((N, wide), lambda j: (0, j)),
            pl.BlockSpec((height, N), lambda j: (0, j // per_group_chunks)),
        ),
        scratch_shapes=[
            pltpu.VMEM((TAIL + height, wide), jnp.float32),
            pltpu.VMEM((height, height), jnp.float32),
            pltpu.VMEM((N, height), jnp.bfloat16),
        ],
        compiler_params=pltpu.CompilerParams(vmem_limit_bytes=32 * 1024 * 1024),
        cost_estimate=pl.CostEstimate(
            flops=2 * height * height * width * CHUNK_HEADS, bytes_accessed=9 * height * width,
            transcendentals=heads * height * height,
        ),
        name="own_block",
    )(x_in, tails, bc_in, tails, z_in, conv_x, conv_bc, cols, rows, skip)

    parts = 2
    state_chunks = 4
    columns = out_weight.shape[1]
    narrow = jnp.bfloat16
    dma = pltpu.SemaphoreType.DMA
    return pl.pallas_call(
        lambda *refs: joined_kernel(size, parts, H * P_SIZE, *refs),
        out_shape=jax.ShapeDtypeStruct((height, columns), narrow),
        in_specs=[pl.BlockSpec(memory_space=pltpu.VMEM)] * 7,
        out_specs=pl.BlockSpec(memory_space=pltpu.VMEM),
        scratch_shapes=[
            pltpu.VMEM((state_chunks, N, width // state_chunks), narrow),
            pltpu.VMEM((state_chunks, N, width // state_chunks), narrow),
            pltpu.VMEM((height, width), jnp.float32),
            pltpu.VMEM((8, height), jnp.float32),
            pltpu.VMEM((size - 1, 8, height), jnp.float32),
            pltpu.VMEM((size, height, width), narrow),
            pltpu.VMEM((size, parts, height // parts, columns), narrow),
            pltpu.VMEM((parts, height // parts, columns), jnp.float32),
            pltpu.VMEM((size - 1, parts, height // parts, columns), narrow),
            pltpu.VMEM((parts, height // parts, columns), narrow),
            dma((state_chunks,)), dma((state_chunks,)),
            dma((size - 1,)), dma((size - 1,)),
            dma((size - 1, parts)), dma((size - 1, parts)),
            dma((size - 1, parts)), dma((size - 1, parts)),
            dma((size, parts)), dma((size - 1, parts)),
            dma((parts,)), dma((parts,)),
        ],
        compiler_params=pltpu.CompilerParams(
            collective_id=0, has_side_effects=True, vmem_limit_bytes=48 * 1024 * 1024
        ),
        cost_estimate=pl.CostEstimate(
            flops=2 * size * height * width * columns, bytes_accessed=9 * height * width,
            transcendentals=0,
        ),
        name="state_norm_project",
    )(p, q, fresh, decay, c_mat, norm_gain[None, :], out_weight)


def from_behind(block, axis, distance):
    devices = range(lax.axis_size(axis))
    route = [(i - distance, i) for i in devices if i - distance in devices]
    return lax.ppermute(block, axis, route)


def conv_with(before, current, weight):
    height = current.shape[0]
    joined = jnp.concatenate([before, current], axis=0).astype(jnp.float32)
    summed = jnp.zeros(current.shape, jnp.float32)
    for offset in range(CONV):
        summed = summed + weight[offset][None, :] * joined[offset : offset + height]
    return summed


def shards(
    x_in, bc_in, z_in, dt_raw, dt_bias, a_log, d_skip, conv_x, conv_bc, norm_gain, out_weight
):
    height = x_in.shape[0]
    heads = dt_raw.shape[1]
    local_width = x_in.shape[1]
    nearby_groups = bc_in.shape[1] // (2 * N)
    per_group = heads // nearby_groups
    tails = from_behind((x_in[height - (CONV - 1) :], bc_in[height - (CONV - 1) :]), "seq", 1)
    input_convolved = jax.nn.silu(conv_with(tails[0], x_in, conv_x)).astype(jnp.bfloat16)
    bc_conv = jax.nn.silu(conv_with(tails[1], bc_in, conv_bc)).astype(jnp.bfloat16)
    step_sizes = jax.nn.softplus(dt_raw + dt_bias[None, :])
    log_decay = -jnp.exp(a_log)[None, :] * step_sizes
    blocks = height // BLOCK
    x_blocks = input_convolved.reshape(blocks, BLOCK, heads, P_SIZE)
    bc_blocks = bc_conv.reshape(blocks, BLOCK, nearby_groups, 2, N)
    b_mat = bc_blocks[:, :, :, 0]
    c_mat = bc_blocks[:, :, :, 1]
    running = jnp.cumsum(log_decay.reshape(blocks, BLOCK, heads), axis=1)
    step_blocks = step_sizes.reshape(blocks, BLOCK, heads)
    places = jnp.arange(BLOCK, dtype=jnp.int32)
    lower = places[:, None] >= places[None, :]

    def inside(input_rows):
        x_here, b_here, c_here, run_here, step_here = input_rows
        scores = jnp.einsum("ign,jgn->gij", c_here, b_here, preferred_element_type=jnp.float32)
        run_heads = run_here.T.reshape(nearby_groups, per_group, BLOCK)
        step_heads = step_here.T.reshape(nearby_groups, per_group, BLOCK)
        spread = run_heads[:, :, :, None] - run_heads[:, :, None, :]
        spread = jnp.where(lower[None, None], spread, -jnp.inf)
        mixing = (scores[:, None] * jnp.exp(spread) * step_heads[:, :, None, :]).astype(
            jnp.bfloat16
        )
        mixing = mixing.reshape(heads, BLOCK, BLOCK)
        within = jnp.einsum("hij,jhp->ihp", mixing, x_here, preferred_element_type=jnp.float32)
        until_finish = jnp.exp(run_here[-1:] - run_here) * step_here
        b_heads = jnp.repeat(b_here.astype(jnp.float32), per_group, axis=1)
        weighted_b = (b_heads * until_finish[:, :, None]).astype(jnp.bfloat16)
        fresh = jnp.einsum("jhn,jhp->hnp", weighted_b, x_here, preferred_element_type=jnp.float32)
        return (within, fresh)

    within, fresh = lax.map(inside, (x_blocks, b_mat, c_mat, running, step_blocks))
    since_beginning = (
        jnp.repeat(c_mat.astype(jnp.float32), per_group, axis=2) * jnp.exp(running)[..., None]
    )
    block_decay = running[:, -1, :]
    state = jnp.zeros((heads, N, P_SIZE), jnp.float32)
    prefix = jnp.zeros((heads,), jnp.float32)
    starts = [state]
    offsets = [prefix]
    state = jnp.exp(block_decay[0])[:, None, None] * state + fresh[0]
    prefix = block_decay[0]
    start_states = jnp.stack(starts)
    start_logs = jnp.stack(offsets)
    totals = lax.all_gather(prefix[None, :], "seq", axis=0, tiled=True)
    ends = jnp.cumsum(totals, axis=0)
    before = jnp.concatenate([jnp.zeros((1, heads), jnp.float32), ends[:-1]], axis=0)
    own_index = lax.axis_index("seq")
    own_before = lax.dynamic_index_in_dim(before, own_index, 0, keepdims=False)
    piece = lax.all_gather(state[None], "seq", axis=0, tiled=True)
    quantity = piece.shape[0]
    reference_point = jnp.arange(quantity, dtype=jnp.int32)
    exponent = jnp.where(
        (reference_point < own_index)[:, None], own_before[None, :] - ends, -jnp.inf
    )
    incoming = jnp.einsum("kh,khnp->hnp", jnp.exp(exponent), piece, precision=lax.Precision.HIGHEST)
    full_starts = start_states + jnp.exp(start_logs)[:, :, None, None] * incoming[None]
    across = jnp.einsum(
        "cihn,chnp->cihp", since_beginning, full_starts, precision=lax.Precision.HIGHEST
    )
    mixed = within + across + d_skip[None, None, :, None] * x_blocks.astype(jnp.float32)
    mixed = mixed.reshape(height, local_width)
    gated = mixed * jax.nn.silu(z_in.astype(jnp.float32))
    square_sums = lax.psum(jnp.sum(gated * gated, axis=1), "head")
    normed = (
        gated * lax.rsqrt(square_sums / (H * P_SIZE) + epsilon)[:, None] * norm_gain[None, :]
    ).astype(jnp.bfloat16)
    terms = jnp.dot(
        normed,
        lax.all_gather(out_weight, "seq", axis=1, tiled=True),
        preferred_element_type=jnp.float32,
    )
    return lax.psum_scatter(terms, "head", scatter_dimension=1, tiled=True).astype(jnp.bfloat16)


def solution(mesh):
    placed = (
        P(("dp", "seq"), "head"),
        P(("dp", "seq"), "head"),
        P(("dp", "seq"), "head"),
        P(("dp", "seq"), "head"),
        P("head"),
        P("head"),
        P("head"),
        P(None, "head"),
        P(None, "head"),
        P("head"),
        P("head", "seq"),
    )
    square = (
        mesh.shape["seq"] == mesh.shape["head"]
        and mesh.shape["seq"] > 1
    )
    return jax.shard_map(
        square_shards if square else shards, mesh=mesh, in_specs=placed, out_specs=P(("dp", "seq"), "head"), check_vma=False
    )
```

```python
import jax
import jax.numpy as jnp
from jax import lax
from jax.experimental import pallas as pl
from jax.experimental.pallas import tpu as pltpu
from jax.sharding import PartitionSpec as P

H = 128
P_SIZE = 64
N = 128
BLOCK = 256
CONV = 4
CHUNK_HEADS = 4
TAIL = 16
MESH = pl.DeviceIdType.MESH


epsilon = 1e-05


def silu(v):
    return v / (1.0 + jnp.exp(-v))


def conv_silu(joined, tail, current, weight):
    height = current.shape[0]
    joined[:TAIL] = tail.astype(jnp.float32)
    joined[TAIL:] = current.astype(jnp.float32)
    summed = weight[0:1] * joined[pl.ds(TAIL - CONV + 1, height)]
    for offset in range(1, CONV):
        summed = summed + weight[offset : offset + 1] * joined[
            pl.ds(TAIL - CONV + 1 + offset, height)
        ]
    return silu(summed).astype(jnp.bfloat16)


def layer_kernel(
    size, channels,
    x_ref, bc_ref, z_ref, dt_ref, bias_ref, log_ref, skip_ref, cx_ref, cbc_ref, gain_ref, w_ref,
    out_ref,
    x_tail, bc_tail, joined, cols, rows, scores, b_turned, c_mats, state_in, state_out,
    sums_out, sums_in, scale_out, scale_in, tokens, total, partial, arrived, final,
    tl_send, tl_recv, st_send, st_recv, ss_send, ss_recv, sc_send, sc_recv,
    up_send, up_recv, dn_send, dn_recv, rs_send, rs_recv, pm_send, pm_recv,
):
    s = lax.axis_index("seq")
    h = lax.axis_index("head")
    height, width = x_ref.shape
    heads = dt_ref.shape[1]
    columns = w_ref.shape[1]
    chunks, wide = tokens.shape[1], tokens.shape[3]
    groups = c_mats.shape[0]
    parts = final.shape[0]
    some = height // parts
    last = size - 1

    def copy(src, dst, send, recv, **where):
        return pltpu.make_async_remote_copy(
            src_ref=src, dst_ref=dst, send_sem=send, recv_sem=recv,
            device_id=where, device_id_type=MESH,
        )

    barrier = pltpu.get_barrier_semaphore()

    def greet(**where):
        pl.semaphore_signal(barrier, inc=1, device_id=where, device_id_type=MESH)

    @pl.when(s > 0)
    def _():
        greet(seq=s - 1)

    @pl.when(s < last)
    def _():
        greet(seq=s + 1)

    for k in range(1, size):
        greet(head=lax.rem(h + k, size))

    @pl.when(s != h)
    def _():
        greet(seq=h, head=s)

    one = jnp.int32(1)
    peers = (
        (size - 1) * one + jnp.where(s > 0, one, 0) + jnp.where(s < last, one, 0)
        + jnp.where(s != h, one, 0)
    )
    pl.semaphore_wait(barrier, peers)

    def tail_copies():
        behind = pl.ds(height - TAIL, TAIL)
        return (
            copy(x_ref.at[behind], x_tail, tl_send.at[0], tl_recv.at[0], seq=s + 1),
            copy(bc_ref.at[behind], bc_tail, tl_send.at[1], tl_recv.at[1], seq=s + 1),
        )

    @pl.when(s < last)
    def _():
        for each in tail_copies():
            each.start()

    @pl.when(s == 0)
    def _():
        x_tail[...] = jnp.zeros_like(x_tail)
        bc_tail[...] = jnp.zeros_like(bc_tail)
        state_in[...] = jnp.zeros_like(state_in)

    lower = lax.broadcasted_iota(jnp.int32, (height, height), 0) >= lax.broadcasted_iota(
        jnp.int32, (height, height), 1
    )
    raw = dt_ref[...] + bias_ref[...]
    steps = jnp.maximum(raw, 0.0) + jnp.log1p(jnp.exp(-jnp.abs(raw)))
    running = jnp.dot(
        jnp.where(lower, 1.0, 0.0), -jnp.exp(log_ref[...]) * steps,
        precision=lax.Precision.HIGHEST, preferred_element_type=jnp.float32,
    )
    until = jnp.exp(running[height - 1 : height] - running) * steps
    skip = jnp.broadcast_to(skip_ref[...], (height, heads))
    turned = jnp.concatenate([running, steps, until, until], axis=1).T
    table = jnp.concatenate([running, skip, until, jnp.exp(running)], axis=1)
    for j in range(chunks):
        low = j * CHUNK_HEADS
        rows[j, :CHUNK_HEADS] = turned[low : low + CHUNK_HEADS]
        rows[j, CHUNK_HEADS:] = turned[heads + low : heads + low + CHUNK_HEADS]
        cols[j] = table if j == 0 else pltpu.roll(table, 4 * heads - low, 1)

    @pl.when(s > 0)
    def _():
        for each in tail_copies():
            each.wait_recv()

    for g in range(groups):
        span = slice(g * 2 * N, (g + 1) * 2 * N)
        bc = conv_silu(joined, bc_tail[:, span], bc_ref[:, span], cbc_ref[:, span])
        b_mat, c_mat = bc[:, :N], bc[:, N:]
        c_mats[g] = c_mat
        b_turned[g] = b_mat.astype(jnp.float32).T.astype(jnp.bfloat16)
        scores[g] = lax.dot_general(
            c_mat, b_mat, (((1,), (1,)), ((), ())), preferred_element_type=jnp.float32
        )

    def state_copy(j):
        return copy(state_out.at[j], state_in.at[j], st_send.at[j], st_recv.at[j], seq=s + 1)

    def up_copy(d, j):
        place = tokens.at[s - d, j]
        return copy(place, place, up_send.at[d, j], up_recv.at[d, j], seq=s + 1)

    def up_landed(d, j):
        place = tokens.at[s - d, j]
        return copy(place, place, up_send.at[d - 1, j], up_recv.at[d - 1, j], seq=s + 1)

    def down_copy(d, j):
        place = tokens.at[s + d, j]
        return copy(place, place, dn_send.at[d, j], dn_recv.at[d, j], seq=s - 1)

    def down_landed(d, j):
        place = tokens.at[s + d, j]
        return copy(place, place, dn_send.at[d - 1, j], dn_recv.at[d - 1, j], seq=s - 1)

    sums_out[...] = jnp.zeros_like(sums_out)

    @pl.loop(0, chunks)
    def _(j):
        g = j // (chunks // groups)
        span = pl.ds(pl.multiple_of(j * wide, wide), wide)
        x = conv_silu(joined, x_tail[:, span], x_ref[:, span], cx_ref[:, span])
        x_wide = x.astype(jnp.float32)
        head_of = lax.broadcasted_iota(jnp.int32, (height, wide), 1) // P_SIZE
        col = cols[j]
        row = rows[j]

        def spread_heads(first):
            value = jnp.broadcast_to(col[:, first : first + 1], (height, wide))
            for k in range(1, CHUNK_HEADS):
                value = jnp.where(head_of == k, col[:, first + k : first + k + 1], value)
            return value

        since = spread_heads(3 * heads)
        fresh = jnp.dot(
            b_turned[g], (x_wide * spread_heads(2 * heads)).astype(jnp.bfloat16),
            preferred_element_type=jnp.float32,
        )

        @pl.when(s == 0)
        def _():
            state_out[j] = fresh.astype(jnp.bfloat16)
            state_copy(j).start()

        mixed = spread_heads(heads) * x_wide
        for k in range(CHUNK_HEADS):
            spread = jnp.where(lower, col[:, k : k + 1] - row[k : k + 1], -jnp.inf)
            mixing = scores[g] * jnp.exp(spread) * row[CHUNK_HEADS + k : CHUNK_HEADS + k + 1]
            mixed = mixed + jnp.dot(
                mixing.astype(jnp.bfloat16),
                jnp.where(head_of == k, x_wide, 0.0).astype(jnp.bfloat16),
                preferred_element_type=jnp.float32,
            )

        @pl.when(s > 0)
        def _():
            state_copy(j).wait_recv()

            @pl.when(s < last)
            def _():
                state_out[j] = (
                    fresh + since[height - 1 : height] * state_in[j].astype(jnp.float32)
                ).astype(jnp.bfloat16)
                state_copy(j).start()

        across = jnp.dot(c_mats[g], state_in[j], preferred_element_type=jnp.float32)
        gated = (mixed + since * across) * silu(z_ref[:, span].astype(jnp.float32))
        tokens[s, j] = (gated * gain_ref[:, span]).astype(jnp.bfloat16)

        @pl.when(s < last)
        def _():
            up_copy(0, j).start()

        @pl.when(s > 0)
        def _():
            down_copy(0, j).start()

        squares = gated * gated
        for k in range(wide // 128):
            sums_out[...] += jnp.sum(
                squares[:, k * 128 : (k + 1) * 128].T, axis=0, keepdims=True
            )

    def sums_copy(k):
        return copy(
            sums_out, sums_in.at[k - 1], ss_send.at[k - 1], ss_recv.at[k - 1],
            head=lax.rem(h + k, size),
        )

    for k in range(1, size):
        sums_copy(k).start()

    def partial_copy(t, r):
        slot = lax.rem(h - t + size, size) - 1
        return copy(
            partial.at[t, r], arrived.at[slot, r], rs_send.at[t, r], rs_recv.at[slot, r], head=t
        )

    def multiply(t, j):
        below = pl.ds(pl.multiple_of(j * wide, wide), wide)
        above = pl.ds(pl.multiple_of((j + 1) * wide, wide), wide)
        for n in range(0, columns, 256):
            span = slice(n, n + 256)
            value = jnp.dot(
                tokens[t, j], w_ref[below, span], preferred_element_type=jnp.float32
            ) + jnp.dot(
                tokens[t, j + 1], w_ref[above, span], preferred_element_type=jnp.float32
            )

            @pl.when(j == 0)
            def _():
                total[t, :, span] = value

            @pl.when(j > 0)
            def _():
                total[t, :, span] += value

    def hand_over(t):
        @pl.when(h != t)
        def _():
            for r in range(parts):
                partial[t, r] = total[t, r * some : (r + 1) * some].astype(jnp.bfloat16)
                partial_copy(t, r).start()

    @pl.loop(0, chunks // 2)
    def _(i):
        multiply(s, 2 * i)

    hand_over(s)

    sums = sums_out[...]
    for k in range(1, size):
        sums_copy(k).wait_recv()
        sums = sums + sums_in[k - 1]
    scale_out[...] = lax.rsqrt(sums / channels + epsilon)

    def scale_copy():
        return copy(scale_out, scale_in, sc_send, sc_recv, seq=h, head=s)

    @pl.when(s != h)
    def _():
        scale_copy().start()

    @pl.when(s == h)
    def _():
        scale_in[...] = scale_out[...]

    for d in range(1, size):
        @pl.loop(0, chunks // 2)
        def _(i):
            for j in (2 * i, 2 * i + 1):
                @pl.when(s - d >= 0)
                def _():
                    up_landed(d, j).wait_recv()
                    if d < last:
                        @pl.when(s < last)
                        def _():
                            up_copy(d, j).start()

                @pl.when(s + d <= last)
                def _():
                    down_landed(d, j).wait_recv()
                    if d < last:
                        @pl.when(s > 0)
                        def _():
                            down_copy(d, j).start()

            @pl.when(s - d >= 0)
            def _():
                multiply(s - d, 2 * i)

            @pl.when(s + d <= last)
            def _():
                multiply(s + d, 2 * i)

        @pl.when(s - d >= 0)
        def _():
            hand_over(s - d)

        @pl.when(s + d <= last)
        def _():
            hand_over(s + d)

    def final_copy(r):
        return copy(
            final.at[r], out_ref.at[pl.ds(r * some, some)], pm_send.at[r], pm_recv.at[r],
            seq=h, head=s,
        )

    @pl.when(s != h)
    def _():
        scale_copy().wait()

    scale = jnp.broadcast_to(scale_in[0:1], (128, height)).T

    for r in range(parts):
        piece = slice(r * some, (r + 1) * some)
        for k in range(1, size):
            copy(
                partial.at[0, r], arrived.at[k - 1, r], rs_send.at[0, r], rs_recv.at[k - 1, r],
                head=lax.rem(h + k, size),
            ).wait_recv()
        for n in range(0, columns, 128):
            span = slice(n, n + 128)
            value = total[h, piece, span]
            for k in range(1, size):
                value = value + arrived[k - 1, r, :, span].astype(jnp.float32)
            final[r, :, span] = (value * scale[piece]).astype(jnp.bfloat16)

        @pl.when(s != h)
        def _():
            final_copy(r).start()

        @pl.when(s == h)
        def _():
            out_ref[piece] = final[r]

    for r in range(parts):
        @pl.when(s != h)
        def _():
            final_copy(r).wait()

    @pl.when(s < last)
    def _():
        for each in tail_copies():
            each.wait_send()

        @pl.loop(0, chunks)
        def _(j):
            state_copy(j).wait_send()

    for k in range(1, size):
        sums_copy(k).wait_send()

    for r in range(parts):
        for t in range(size):
            @pl.when(h != t)
            def _():
                partial_copy(t, r).wait_send()

    for d in range(last):
        @pl.when((s < last) & (s - d >= 0))
        def _():
            @pl.loop(0, chunks)
            def _(j):
                up_copy(d, j).wait_send()

        @pl.when((s > 0) & (s + d <= last))
        def _():
            @pl.loop(0, chunks)
            def _(j):
                down_copy(d, j).wait_send()


def square_shards(
    x_in, bc_in, z_in, dt_raw, dt_bias, a_log, d_skip, conv_x, conv_bc, norm_gain, out_weight
):
    size = lax.axis_size("seq")
    height, width = x_in.shape
    heads = dt_raw.shape[1]
    groups = bc_in.shape[1] // (2 * N)
    chunks = heads // CHUNK_HEADS
    wide = CHUNK_HEADS * P_SIZE
    columns = out_weight.shape[1]
    parts = 2
    some = height // parts
    narrow = jnp.bfloat16
    dma = pltpu.SemaphoreType.DMA
    operands = (
        x_in, bc_in, z_in, dt_raw, dt_bias[None, :], a_log[None, :], d_skip[None, :],
        conv_x, conv_bc, norm_gain[None, :], out_weight,
    )
    return pl.pallas_call(
        lambda *refs: layer_kernel(size, H * P_SIZE, *refs),
        out_shape=jax.ShapeDtypeStruct((height, columns), narrow),
        in_specs=[pl.BlockSpec(memory_space=pltpu.VMEM)] * len(operands),
        out_specs=pl.BlockSpec(memory_space=pltpu.VMEM),
        scratch_shapes=[
            pltpu.VMEM((TAIL, width), narrow),
            pltpu.VMEM((TAIL, groups * 2 * N), narrow),
            pltpu.VMEM((TAIL + height, wide), jnp.float32),
            pltpu.VMEM((chunks, height, 4 * heads), jnp.float32),
            pltpu.VMEM((chunks, 2 * CHUNK_HEADS, height), jnp.float32),
            pltpu.VMEM((groups, height, height), jnp.float32),
            pltpu.VMEM((groups, N, height), narrow),
            pltpu.VMEM((groups, height, N), narrow),
            pltpu.VMEM((chunks, N, wide), narrow),
            pltpu.VMEM((chunks, N, wide), narrow),
            pltpu.VMEM((8, height), jnp.float32),
            pltpu.VMEM((size - 1, 8, height), jnp.float32),
            pltpu.VMEM((8, height), jnp.float32),
            pltpu.VMEM((8, height), jnp.float32),
            pltpu.VMEM((size, chunks, height, wide), narrow),
            pltpu.VMEM((size, height, columns), jnp.float32),
            pltpu.VMEM((size, parts, some, columns), narrow),
            pltpu.VMEM((size - 1, parts, some, columns), narrow),
            pltpu.VMEM((parts, some, columns), narrow),
            dma((2,)), dma((2,)),
            dma((chunks,)), dma((chunks,)),
            dma((size - 1,)), dma((size - 1,)),
            dma, dma,
            dma((size - 1, chunks)), dma((size - 1, chunks)),
            dma((size - 1, chunks)), dma((size - 1, chunks)),
            dma((size, parts)), dma((size - 1, parts)),
            dma((parts,)), dma((parts,)),
        ],
        compiler_params=pltpu.CompilerParams(
            collective_id=0, has_side_effects=True, vmem_limit_bytes=52 * 1024 * 1024
        ),
        cost_estimate=pl.CostEstimate(
            flops=2 * size * height * width * columns, bytes_accessed=9 * height * width,
            transcendentals=heads * height * height,
        ),
        name="layer",
    )(*operands)


def from_behind(block, axis, distance):
    devices = range(lax.axis_size(axis))
    route = [(i - distance, i) for i in devices if i - distance in devices]
    return lax.ppermute(block, axis, route)


def conv_with(before, current, weight):
    height = current.shape[0]
    joined = jnp.concatenate([before, current], axis=0).astype(jnp.float32)
    summed = jnp.zeros(current.shape, jnp.float32)
    for offset in range(CONV):
        summed = summed + weight[offset][None, :] * joined[offset : offset + height]
    return summed


def shards(
    x_in, bc_in, z_in, dt_raw, dt_bias, a_log, d_skip, conv_x, conv_bc, norm_gain, out_weight
):
    height = x_in.shape[0]
    heads = dt_raw.shape[1]
    local_width = x_in.shape[1]
    nearby_groups = bc_in.shape[1] // (2 * N)
    per_group = heads // nearby_groups
    tails = from_behind((x_in[height - (CONV - 1) :], bc_in[height - (CONV - 1) :]), "seq", 1)
    input_convolved = jax.nn.silu(conv_with(tails[0], x_in, conv_x)).astype(jnp.bfloat16)
    bc_conv = jax.nn.silu(conv_with(tails[1], bc_in, conv_bc)).astype(jnp.bfloat16)
    step_sizes = jax.nn.softplus(dt_raw + dt_bias[None, :])
    log_decay = -jnp.exp(a_log)[None, :] * step_sizes
    blocks = height // BLOCK
    x_blocks = input_convolved.reshape(blocks, BLOCK, heads, P_SIZE)
    bc_blocks = bc_conv.reshape(blocks, BLOCK, nearby_groups, 2, N)
    b_mat = bc_blocks[:, :, :, 0]
    c_mat = bc_blocks[:, :, :, 1]
    running = jnp.cumsum(log_decay.reshape(blocks, BLOCK, heads), axis=1)
    step_blocks = step_sizes.reshape(blocks, BLOCK, heads)
    places = jnp.arange(BLOCK, dtype=jnp.int32)
    lower = places[:, None] >= places[None, :]

    def inside(input_rows):
        x_here, b_here, c_here, run_here, step_here = input_rows
        scores = jnp.einsum("ign,jgn->gij", c_here, b_here, preferred_element_type=jnp.float32)
        run_heads = run_here.T.reshape(nearby_groups, per_group, BLOCK)
        step_heads = step_here.T.reshape(nearby_groups, per_group, BLOCK)
        spread = run_heads[:, :, :, None] - run_heads[:, :, None, :]
        spread = jnp.where(lower[None, None], spread, -jnp.inf)
        mixing = (scores[:, None] * jnp.exp(spread) * step_heads[:, :, None, :]).astype(
            jnp.bfloat16
        )
        mixing = mixing.reshape(heads, BLOCK, BLOCK)
        within = jnp.einsum("hij,jhp->ihp", mixing, x_here, preferred_element_type=jnp.float32)
        until_finish = jnp.exp(run_here[-1:] - run_here) * step_here
        b_heads = jnp.repeat(b_here.astype(jnp.float32), per_group, axis=1)
        weighted_b = (b_heads * until_finish[:, :, None]).astype(jnp.bfloat16)
        fresh = jnp.einsum("jhn,jhp->hnp", weighted_b, x_here, preferred_element_type=jnp.float32)
        return (within, fresh)

    within, fresh = lax.map(inside, (x_blocks, b_mat, c_mat, running, step_blocks))
    since_beginning = (
        jnp.repeat(c_mat.astype(jnp.float32), per_group, axis=2) * jnp.exp(running)[..., None]
    )
    block_decay = running[:, -1, :]
    state = jnp.zeros((heads, N, P_SIZE), jnp.float32)
    prefix = jnp.zeros((heads,), jnp.float32)
    starts = [state]
    offsets = [prefix]
    state = jnp.exp(block_decay[0])[:, None, None] * state + fresh[0]
    prefix = block_decay[0]
    start_states = jnp.stack(starts)
    start_logs = jnp.stack(offsets)
    totals = lax.all_gather(prefix[None, :], "seq", axis=0, tiled=True)
    ends = jnp.cumsum(totals, axis=0)
    before = jnp.concatenate([jnp.zeros((1, heads), jnp.float32), ends[:-1]], axis=0)
    own_index = lax.axis_index("seq")
    own_before = lax.dynamic_index_in_dim(before, own_index, 0, keepdims=False)
    piece = lax.all_gather(state[None], "seq", axis=0, tiled=True)
    quantity = piece.shape[0]
    reference_point = jnp.arange(quantity, dtype=jnp.int32)
    exponent = jnp.where(
        (reference_point < own_index)[:, None], own_before[None, :] - ends, -jnp.inf
    )
    incoming = jnp.einsum("kh,khnp->hnp", jnp.exp(exponent), piece, precision=lax.Precision.HIGHEST)
    full_starts = start_states + jnp.exp(start_logs)[:, :, None, None] * incoming[None]
    across = jnp.einsum(
        "cihn,chnp->cihp", since_beginning, full_starts, precision=lax.Precision.HIGHEST
    )
    mixed = within + across + d_skip[None, None, :, None] * x_blocks.astype(jnp.float32)
    mixed = mixed.reshape(height, local_width)
    gated = mixed * jax.nn.silu(z_in.astype(jnp.float32))
    square_sums = lax.psum(jnp.sum(gated * gated, axis=1), "head")
    normed = (
        gated * lax.rsqrt(square_sums / (H * P_SIZE) + epsilon)[:, None] * norm_gain[None, :]
    ).astype(jnp.bfloat16)
    terms = jnp.dot(
        normed,
        lax.all_gather(out_weight, "seq", axis=1, tiled=True),
        preferred_element_type=jnp.float32,
    )
    return lax.psum_scatter(terms, "head", scatter_dimension=1, tiled=True).astype(jnp.bfloat16)


def solution(mesh):
    placed = (
        P(("dp", "seq"), "head"),
        P(("dp", "seq"), "head"),
        P(("dp", "seq"), "head"),
        P(("dp", "seq"), "head"),
        P("head"),
        P("head"),
        P("head"),
        P(None, "head"),
        P(None, "head"),
        P("head"),
        P("head", "seq"),
    )
    square = (
        mesh.shape["seq"] == mesh.shape["head"]
        and mesh.shape["seq"] > 1
    )
    return jax.shard_map(
        square_shards if square else shards, mesh=mesh, in_specs=placed, out_specs=P(("dp", "seq"), "head"), check_vma=False
    )
```

```python
import jax
import jax.numpy as jnp
from jax import lax
from jax.experimental import pallas as pl
from jax.experimental.pallas import tpu as pltpu
from jax.sharding import PartitionSpec as P

H = 128
P_SIZE = 64
N = 128
BLOCK = 256
CONV = 4
CHUNK_HEADS = 4
TAIL = 16
MESH = pl.DeviceIdType.MESH


epsilon = 1e-05


def silu(v):
    return v / (1.0 + jnp.exp(-v))


def conv_silu(joined, tail, current, weight):
    height = current.shape[0]
    joined[:TAIL] = tail.astype(jnp.float32)
    joined[TAIL:] = current.astype(jnp.float32)
    summed = weight[0:1] * joined[pl.ds(TAIL - CONV + 1, height)]
    for offset in range(1, CONV):
        summed = summed + weight[offset : offset + 1] * joined[
            pl.ds(TAIL - CONV + 1 + offset, height)
        ]
    return silu(summed).astype(jnp.bfloat16)


def layer_kernel(
    size, channels,
    x_ref, bc_ref, z_ref, dt_ref, bias_ref, log_ref, skip_ref, cx_ref, cbc_ref, gain_ref, w_ref,
    out_ref,
    x_tail, bc_tail, joined, cols, rows, scores, b_turned, c_mats, state_in, state_out,
    sums_out, sums_in, scale_out, scale_in, tokens, total, partial, arrived, final, passing,
    scale_cols,
    tl_send, tl_recv, st_send, st_recv, ss_send, ss_recv, sc_send, sc_recv,
    up_send, up_recv, dn_send, dn_recv, rs_send, rs_recv, al_send, al_recv, pm_send, pm_recv,
):
    s = lax.axis_index("seq")
    h = lax.axis_index("head")
    height, width = x_ref.shape
    heads = dt_ref.shape[1]
    columns = w_ref.shape[1]
    chunks, wide = tokens.shape[1], tokens.shape[3]
    groups = c_mats.shape[0]
    parts = final.shape[0]
    some = height // parts
    last = size - 1

    def copy(src, dst, send, recv, **where):
        return pltpu.make_async_remote_copy(
            src_ref=src, dst_ref=dst, send_sem=send, recv_sem=recv,
            device_id=where, device_id_type=MESH,
        )

    barrier = pltpu.get_barrier_semaphore()

    def greet(**where):
        pl.semaphore_signal(barrier, inc=1, device_id=where, device_id_type=MESH)

    for k in range(1, size):
        greet(seq=lax.rem(s + k, size))
        greet(head=lax.rem(h + k, size))
    pl.semaphore_wait(barrier, 2 * (size - 1))

    mate = lax.rem(h - s + size, size)
    apart = jnp.maximum(mate - s, s - mate)

    def tail_copies():
        behind = pl.ds(height - TAIL, TAIL)
        return (
            copy(x_ref.at[behind], x_tail, tl_send.at[0], tl_recv.at[0], seq=s + 1),
            copy(bc_ref.at[behind], bc_tail, tl_send.at[1], tl_recv.at[1], seq=s + 1),
        )

    @pl.when(s < last)
    def _():
        for each in tail_copies():
            each.start()

    @pl.when(s == 0)
    def _():
        x_tail[...] = jnp.zeros_like(x_tail)
        bc_tail[...] = jnp.zeros_like(bc_tail)
        state_in[...] = jnp.zeros_like(state_in)

    lower = lax.broadcasted_iota(jnp.int32, (height, height), 0) >= lax.broadcasted_iota(
        jnp.int32, (height, height), 1
    )
    raw = dt_ref[...] + bias_ref[...]
    steps = jnp.maximum(raw, 0.0) + jnp.log1p(jnp.exp(-jnp.abs(raw)))
    running = jnp.dot(
        jnp.where(lower, 1.0, 0.0), -jnp.exp(log_ref[...]) * steps,
        precision=lax.Precision.HIGHEST, preferred_element_type=jnp.float32,
    )
    until = jnp.exp(running[height - 1 : height] - running) * steps
    skip = jnp.broadcast_to(skip_ref[...], (height, heads))
    turned = jnp.concatenate([running, steps, until, until], axis=1).T
    table = jnp.concatenate([running, skip, until, jnp.exp(running)], axis=1)
    for j in range(chunks):
        low = j * CHUNK_HEADS
        rows[j, :CHUNK_HEADS] = turned[low : low + CHUNK_HEADS]
        rows[j, CHUNK_HEADS:] = turned[heads + low : heads + low + CHUNK_HEADS]
        cols[j] = table if j == 0 else pltpu.roll(table, 4 * heads - low, 1)

    @pl.when(s > 0)
    def _():
        for each in tail_copies():
            each.wait_recv()

    for g in range(groups):
        span = slice(g * 2 * N, (g + 1) * 2 * N)
        bc = conv_silu(joined, bc_tail[:, span], bc_ref[:, span], cbc_ref[:, span])
        b_mat, c_mat = bc[:, :N], bc[:, N:]
        c_mats[g] = c_mat
        b_turned[g] = b_mat.astype(jnp.float32).T.astype(jnp.bfloat16)
        scores[g] = lax.dot_general(
            c_mat, b_mat, (((1,), (1,)), ((), ())), preferred_element_type=jnp.float32
        )

    def state_copy(j):
        return copy(state_out.at[j], state_in.at[j], st_send.at[j], st_recv.at[j], seq=s + 1)

    def up_copy(d, j):
        place = tokens.at[s - d, j]
        return copy(place, place, up_send.at[d, j], up_recv.at[d, j], seq=s + 1)

    def up_landed(d, j):
        place = tokens.at[s - d, j]
        return copy(place, place, up_send.at[d - 1, j], up_recv.at[d - 1, j], seq=s + 1)

    def down_copy(d, j):
        place = tokens.at[s + d, j]
        return copy(place, place, dn_send.at[d, j], dn_recv.at[d, j], seq=s - 1)

    def down_landed(d, j):
        place = tokens.at[s + d, j]
        return copy(place, place, dn_send.at[d - 1, j], dn_recv.at[d - 1, j], seq=s - 1)

    sums_out[...] = jnp.zeros_like(sums_out)

    @pl.loop(0, chunks)
    def _(j):
        g = j // (chunks // groups)
        span = pl.ds(pl.multiple_of(j * wide, wide), wide)
        x = conv_silu(joined, x_tail[:, span], x_ref[:, span], cx_ref[:, span])
        x_wide = x.astype(jnp.float32)
        head_of = lax.broadcasted_iota(jnp.int32, (height, wide), 1) // P_SIZE
        col = cols[j]
        row = rows[j]

        def spread_heads(first):
            value = jnp.broadcast_to(col[:, first : first + 1], (height, wide))
            for k in range(1, CHUNK_HEADS):
                value = jnp.where(head_of == k, col[:, first + k : first + k + 1], value)
            return value

        since = spread_heads(3 * heads)
        fresh = jnp.dot(
            b_turned[g], (x_wide * spread_heads(2 * heads)).astype(jnp.bfloat16),
            preferred_element_type=jnp.float32,
        )

        @pl.when(s == 0)
        def _():
            state_out[j] = fresh.astype(jnp.bfloat16)
            state_copy(j).start()

        mixed = spread_heads(heads) * x_wide
        for k in range(CHUNK_HEADS):
            spread = jnp.where(lower, col[:, k : k + 1] - row[k : k + 1], -jnp.inf)
            mixing = scores[g] * jnp.exp(spread) * row[CHUNK_HEADS + k : CHUNK_HEADS + k + 1]
            mixed = mixed + jnp.dot(
                mixing.astype(jnp.bfloat16),
                jnp.where(head_of == k, x_wide, 0.0).astype(jnp.bfloat16),
                preferred_element_type=jnp.float32,
            )

        @pl.when(s > 0)
        def _():
            state_copy(j).wait_recv()

            @pl.when(s < last)
            def _():
                state_out[j] = (
                    fresh + since[height - 1 : height] * state_in[j].astype(jnp.float32)
                ).astype(jnp.bfloat16)
                state_copy(j).start()

        across = jnp.dot(c_mats[g], state_in[j], preferred_element_type=jnp.float32)
        gated = (mixed + since * across) * silu(z_ref[:, span].astype(jnp.float32))
        tokens[s, j] = (gated * gain_ref[:, span]).astype(jnp.bfloat16)

        @pl.when(s < last)
        def _():
            up_copy(0, j).start()

        @pl.when(s > 0)
        def _():
            down_copy(0, j).start()

        squares = gated * gated
        for k in range(wide // 128):
            sums_out[...] += jnp.sum(
                squares[:, k * 128 : (k + 1) * 128].T, axis=0, keepdims=True
            )

    def sums_copy(k):
        return copy(
            sums_out, sums_in.at[k - 1], ss_send.at[k - 1], ss_recv.at[k - 1],
            head=lax.rem(h + k, size),
        )

    for k in range(1, size):
        sums_copy(k).start()

    def partial_copy(t, r):
        adder = lax.rem(t + s, size)
        slot = lax.rem(h - adder + size, size) - 1
        return copy(
            partial.at[t, r], arrived.at[slot, r], rs_send.at[t, r], rs_recv.at[slot, r],
            head=adder,
        )

    def multiply(t, j):
        below = pl.ds(pl.multiple_of(j * wide, wide), wide)
        above = pl.ds(pl.multiple_of((j + 1) * wide, wide), wide)
        for n in range(0, columns, 256):
            span = slice(n, n + 256)
            value = jnp.dot(
                tokens[t, j], w_ref[below, span], preferred_element_type=jnp.float32
            ) + jnp.dot(
                tokens[t, j + 1], w_ref[above, span], preferred_element_type=jnp.float32
            )

            @pl.when(j == 0)
            def _():
                total[t, :, span] = value

            @pl.when(j > 0)
            def _():
                total[t, :, span] += value

    def hand_over(t):
        @pl.when(mate != t)
        def _():
            @pl.loop(0, parts)
            def _(r):
                piece = pl.ds(pl.multiple_of(r * some, some), some)
                partial[t, r] = total[t, piece].astype(jnp.bfloat16)
                partial_copy(t, r).start()

    @pl.loop(0, chunks // 2)
    def _(i):
        multiply(s, 2 * i)

    hand_over(s)

    sums = sums_out[...]
    for k in range(1, size):
        sums_copy(k).wait_recv()
        sums = sums + sums_in[k - 1]
    scale_out[...] = lax.rsqrt(sums / channels + epsilon)

    def scale_copy():
        return copy(scale_out, scale_in, sc_send, sc_recv, seq=mate)

    @pl.when(s != mate)
    def _():
        scale_copy().start()

    @pl.when(s == mate)
    def _():
        scale_in[...] = scale_out[...]

    def along_copy(r):
        return copy(final.at[r], passing.at[r], al_send.at[r], al_recv.at[r], seq=mate)

    def across_copy(r):
        place = out_ref.at[pl.ds(r * some, some)]
        return copy(passing.at[r], place, pm_send.at[r], pm_recv.at[r], head=mate)

    def collect():
        @pl.when(s != mate)
        def _():
            scale_copy().wait()

        scale_cols[...] = jnp.broadcast_to(scale_in[0:1], (128, height)).T

        @pl.loop(0, parts)
        def _(r):
            piece = pl.ds(pl.multiple_of(r * some, some), some)
            for k in range(1, size):
                copy(
                    partial.at[0, r], arrived.at[k - 1, r], rs_send.at[0, r],
                    rs_recv.at[k - 1, r], head=lax.rem(h + k, size),
                ).wait_recv()
            for n in range(0, columns, 128):
                span = slice(n, n + 128)
                value = total[mate, piece, span]
                for k in range(1, size):
                    value = value + arrived[k - 1, r, :, span].astype(jnp.float32)
                final[r, :, span] = (value * scale_cols[piece, :]).astype(jnp.bfloat16)

            @pl.when(s != mate)
            def _():
                along_copy(r).start()

            @pl.when(s == mate)
            def _():
                passing[r] = final[r]

    def deliver():
        @pl.loop(0, parts)
        def _(r):
            @pl.when(s != mate)
            def _():
                along_copy(r).wait_recv()

            @pl.when(s > 0)
            def _():
                across_copy(r).start()

            @pl.when(s == 0)
            def _():
                out_ref[pl.ds(pl.multiple_of(r * some, some), some)] = passing[r]

    for d in range(1, size):
        @pl.loop(0, chunks // 2)
        def _(i):
            for j in (2 * i, 2 * i + 1):
                @pl.when(s - d >= 0)
                def _():
                    up_landed(d, j).wait_recv()
                    if d < last:
                        @pl.when(s < last)
                        def _():
                            up_copy(d, j).start()

                @pl.when(s + d <= last)
                def _():
                    down_landed(d, j).wait_recv()
                    if d < last:
                        @pl.when(s > 0)
                        def _():
                            down_copy(d, j).start()

            @pl.when(s - d >= 0)
            def _():
                multiply(s - d, 2 * i)

            @pl.when(s + d <= last)
            def _():
                multiply(s + d, 2 * i)

        @pl.when(s - d >= 0)
        def _():
            hand_over(s - d)

        @pl.when(s + d <= last)
        def _():
            hand_over(s + d)

        @pl.when(apart == d - 1)
        def _():
            collect()

        if d > 1:
            @pl.when(apart == d - 2)
            def _():
                deliver()

    @pl.when(apart == last)
    def _():
        collect()

    @pl.when(apart >= last - 1)
    def _():
        deliver()

    @pl.loop(0, parts)
    def _(r):
        @pl.when(s != mate)
        def _():
            along_copy(r).wait_send()

        @pl.when(s > 0)
        def _():
            across_copy(r).wait()

    @pl.when(s < last)
    def _():
        for each in tail_copies():
            each.wait_send()

        @pl.loop(0, chunks)
        def _(j):
            state_copy(j).wait_send()

    for k in range(1, size):
        sums_copy(k).wait_send()

    for t in range(size):
        @pl.when(mate != t)
        def _():
            @pl.loop(0, parts)
            def _(r):
                partial_copy(t, r).wait_send()

    for d in range(last):
        @pl.when((s < last) & (s - d >= 0))
        def _():
            @pl.loop(0, chunks)
            def _(j):
                up_copy(d, j).wait_send()

        @pl.when((s > 0) & (s + d <= last))
        def _():
            @pl.loop(0, chunks)
            def _(j):
                down_copy(d, j).wait_send()


def square_shards(
    x_in, bc_in, z_in, dt_raw, dt_bias, a_log, d_skip, conv_x, conv_bc, norm_gain, out_weight
):
    size = lax.axis_size("seq")
    height, width = x_in.shape
    heads = dt_raw.shape[1]
    groups = bc_in.shape[1] // (2 * N)
    chunks = heads // CHUNK_HEADS
    wide = CHUNK_HEADS * P_SIZE
    columns = out_weight.shape[1]
    parts = 4
    some = height // parts
    narrow = jnp.bfloat16
    dma = pltpu.SemaphoreType.DMA
    operands = (
        x_in, bc_in, z_in, dt_raw, dt_bias[None, :], a_log[None, :], d_skip[None, :],
        conv_x, conv_bc, norm_gain[None, :], out_weight,
    )
    return pl.pallas_call(
        lambda *refs: layer_kernel(size, H * P_SIZE, *refs),
        out_shape=jax.ShapeDtypeStruct((height, columns), narrow),
        in_specs=[pl.BlockSpec(memory_space=pltpu.VMEM)] * len(operands),
        out_specs=pl.BlockSpec(memory_space=pltpu.VMEM),
        scratch_shapes=[
            pltpu.VMEM((TAIL, width), narrow),
            pltpu.VMEM((TAIL, groups * 2 * N), narrow),
            pltpu.VMEM((TAIL + height, wide), jnp.float32),
            pltpu.VMEM((chunks, height, 4 * heads), jnp.float32),
            pltpu.VMEM((chunks, 2 * CHUNK_HEADS, height), jnp.float32),
            pltpu.VMEM((groups, height, height), jnp.float32),
            pltpu.VMEM((groups, N, height), narrow),
            pltpu.VMEM((groups, height, N), narrow),
            pltpu.VMEM((chunks, N, wide), narrow),
            pltpu.VMEM((chunks, N, wide), narrow),
            pltpu.VMEM((8, height), jnp.float32),
            pltpu.VMEM((size - 1, 8, height), jnp.float32),
            pltpu.VMEM((8, height), jnp.float32),
            pltpu.VMEM((8, height), jnp.float32),
            pltpu.VMEM((size, chunks, height, wide), narrow),
            pltpu.VMEM((size, height, columns), jnp.float32),
            pltpu.VMEM((size, parts, some, columns), narrow),
            pltpu.VMEM((size - 1, parts, some, columns), narrow),
            pltpu.VMEM((parts, some, columns), narrow),
            pltpu.VMEM((parts, some, columns), narrow),
            pltpu.VMEM((height, 128), jnp.float32),
            dma((2,)), dma((2,)),
            dma((chunks,)), dma((chunks,)),
            dma((size - 1,)), dma((size - 1,)),
            dma, dma,
            dma((size - 1, chunks)), dma((size - 1, chunks)),
            dma((size - 1, chunks)), dma((size - 1, chunks)),
            dma((size, parts)), dma((size - 1, parts)),
            dma((parts,)), dma((parts,)),
            dma((parts,)), dma((parts,)),
        ],
        compiler_params=pltpu.CompilerParams(
            collective_id=0, has_side_effects=True, vmem_limit_bytes=52 * 1024 * 1024
        ),
        cost_estimate=pl.CostEstimate(
            flops=2 * size * height * width * columns, bytes_accessed=9 * height * width,
            transcendentals=heads * height * height,
        ),
        name="layer",
    )(*operands)


def from_behind(block, axis, distance):
    devices = range(lax.axis_size(axis))
    route = [(i - distance, i) for i in devices if i - distance in devices]
    return lax.ppermute(block, axis, route)


def conv_with(before, current, weight):
    height = current.shape[0]
    joined = jnp.concatenate([before, current], axis=0).astype(jnp.float32)
    summed = jnp.zeros(current.shape, jnp.float32)
    for offset in range(CONV):
        summed = summed + weight[offset][None, :] * joined[offset : offset + height]
    return summed


def shards(
    x_in, bc_in, z_in, dt_raw, dt_bias, a_log, d_skip, conv_x, conv_bc, norm_gain, out_weight
):
    height = x_in.shape[0]
    heads = dt_raw.shape[1]
    local_width = x_in.shape[1]
    nearby_groups = bc_in.shape[1] // (2 * N)
    per_group = heads // nearby_groups
    tails = from_behind((x_in[height - (CONV - 1) :], bc_in[height - (CONV - 1) :]), "seq", 1)
    input_convolved = jax.nn.silu(conv_with(tails[0], x_in, conv_x)).astype(jnp.bfloat16)
    bc_conv = jax.nn.silu(conv_with(tails[1], bc_in, conv_bc)).astype(jnp.bfloat16)
    step_sizes = jax.nn.softplus(dt_raw + dt_bias[None, :])
    log_decay = -jnp.exp(a_log)[None, :] * step_sizes
    blocks = height // BLOCK
    x_blocks = input_convolved.reshape(blocks, BLOCK, heads, P_SIZE)
    bc_blocks = bc_conv.reshape(blocks, BLOCK, nearby_groups, 2, N)
    b_mat = bc_blocks[:, :, :, 0]
    c_mat = bc_blocks[:, :, :, 1]
    running = jnp.cumsum(log_decay.reshape(blocks, BLOCK, heads), axis=1)
    step_blocks = step_sizes.reshape(blocks, BLOCK, heads)
    places = jnp.arange(BLOCK, dtype=jnp.int32)
    lower = places[:, None] >= places[None, :]

    def inside(input_rows):
        x_here, b_here, c_here, run_here, step_here = input_rows
        scores = jnp.einsum("ign,jgn->gij", c_here, b_here, preferred_element_type=jnp.float32)
        run_heads = run_here.T.reshape(nearby_groups, per_group, BLOCK)
        step_heads = step_here.T.reshape(nearby_groups, per_group, BLOCK)
        spread = run_heads[:, :, :, None] - run_heads[:, :, None, :]
        spread = jnp.where(lower[None, None], spread, -jnp.inf)
        mixing = (scores[:, None] * jnp.exp(spread) * step_heads[:, :, None, :]).astype(
            jnp.bfloat16
        )
        mixing = mixing.reshape(heads, BLOCK, BLOCK)
        within = jnp.einsum("hij,jhp->ihp", mixing, x_here, preferred_element_type=jnp.float32)
        until_finish = jnp.exp(run_here[-1:] - run_here) * step_here
        b_heads = jnp.repeat(b_here.astype(jnp.float32), per_group, axis=1)
        weighted_b = (b_heads * until_finish[:, :, None]).astype(jnp.bfloat16)
        fresh = jnp.einsum("jhn,jhp->hnp", weighted_b, x_here, preferred_element_type=jnp.float32)
        return (within, fresh)

    within, fresh = lax.map(inside, (x_blocks, b_mat, c_mat, running, step_blocks))
    since_beginning = (
        jnp.repeat(c_mat.astype(jnp.float32), per_group, axis=2) * jnp.exp(running)[..., None]
    )
    block_decay = running[:, -1, :]
    state = jnp.zeros((heads, N, P_SIZE), jnp.float32)
    prefix = jnp.zeros((heads,), jnp.float32)
    starts = [state]
    offsets = [prefix]
    state = jnp.exp(block_decay[0])[:, None, None] * state + fresh[0]
    prefix = block_decay[0]
    start_states = jnp.stack(starts)
    start_logs = jnp.stack(offsets)
    totals = lax.all_gather(prefix[None, :], "seq", axis=0, tiled=True)
    ends = jnp.cumsum(totals, axis=0)
    before = jnp.concatenate([jnp.zeros((1, heads), jnp.float32), ends[:-1]], axis=0)
    own_index = lax.axis_index("seq")
    own_before = lax.dynamic_index_in_dim(before, own_index, 0, keepdims=False)
    piece = lax.all_gather(state[None], "seq", axis=0, tiled=True)
    quantity = piece.shape[0]
    reference_point = jnp.arange(quantity, dtype=jnp.int32)
    exponent = jnp.where(
        (reference_point < own_index)[:, None], own_before[None, :] - ends, -jnp.inf
    )
    incoming = jnp.einsum("kh,khnp->hnp", jnp.exp(exponent), piece, precision=lax.Precision.HIGHEST)
    full_starts = start_states + jnp.exp(start_logs)[:, :, None, None] * incoming[None]
    across = jnp.einsum(
        "cihn,chnp->cihp", since_beginning, full_starts, precision=lax.Precision.HIGHEST
    )
    mixed = within + across + d_skip[None, None, :, None] * x_blocks.astype(jnp.float32)
    mixed = mixed.reshape(height, local_width)
    gated = mixed * jax.nn.silu(z_in.astype(jnp.float32))
    square_sums = lax.psum(jnp.sum(gated * gated, axis=1), "head")
    normed = (
        gated * lax.rsqrt(square_sums / (H * P_SIZE) + epsilon)[:, None] * norm_gain[None, :]
    ).astype(jnp.bfloat16)
    terms = jnp.dot(
        normed,
        lax.all_gather(out_weight, "seq", axis=1, tiled=True),
        preferred_element_type=jnp.float32,
    )
    return lax.psum_scatter(terms, "head", scatter_dimension=1, tiled=True).astype(jnp.bfloat16)


def solution(mesh):
    placed = (
        P(("dp", "seq"), "head"),
        P(("dp", "seq"), "head"),
        P(("dp", "seq"), "head"),
        P(("dp", "seq"), "head"),
        P("head"),
        P("head"),
        P("head"),
        P(None, "head"),
        P(None, "head"),
        P("head"),
        P("head", "seq"),
    )
    square = (
        mesh.shape["seq"] == mesh.shape["head"]
        and mesh.shape["seq"] > 1
    )
    return jax.shard_map(
        square_shards if square else shards, mesh=mesh, in_specs=placed, out_specs=P(("dp", "seq"), "head"), check_vma=False
    )
```

```python
import jax
import jax.numpy as jnp
from jax import lax
from jax.experimental import pallas as pl
from jax.experimental.pallas import tpu as pltpu
from jax.sharding import PartitionSpec as P

H = 128
P_SIZE = 64
N = 128
BLOCK = 256
CONV = 4
CHUNK_HEADS = 4
TAIL = 16
MESH = pl.DeviceIdType.MESH


epsilon = 1e-05


def silu(v):
    return v / (1.0 + jnp.exp(-v))


def conv_silu(joined, tail, current, weight):
    height = current.shape[0]
    joined[:TAIL] = tail.astype(jnp.float32)
    joined[TAIL:] = current.astype(jnp.float32)
    summed = weight[0:1] * joined[pl.ds(TAIL - CONV + 1, height)]
    for offset in range(1, CONV):
        summed = summed + weight[offset : offset + 1] * joined[
            pl.ds(TAIL - CONV + 1 + offset, height)
        ]
    return silu(summed).astype(jnp.bfloat16)


def layer_kernel(
    size, channels,
    x_ref, bc_ref, z_ref, dt_ref, bias_ref, log_ref, skip_ref, cx_ref, cbc_ref, gain_ref, w_ref,
    out_ref,
    x_tail, bc_tail, joined, cols, rows, scores, b_turned, c_mats, state_in, state_out,
    sums_out, sums_in, scale_out, scale_in, tokens, total, partial, arrived, final, passing,
    scale_cols,
    tl_send, tl_recv, st_send, st_recv, ss_send, ss_recv, sc_send, sc_recv,
    up_send, up_recv, dn_send, dn_recv, rs_send, rs_recv, al_send, al_recv, pm_send, pm_recv,
):
    s = lax.axis_index("seq")
    h = lax.axis_index("head")
    height, width = x_ref.shape
    heads = dt_ref.shape[1]
    columns = w_ref.shape[1]
    chunks, wide = tokens.shape[1], tokens.shape[3]
    groups = c_mats.shape[0]
    parts = final.shape[0]
    some = height // parts
    last = size - 1

    def copy(src, dst, send, recv, **where):
        return pltpu.make_async_remote_copy(
            src_ref=src, dst_ref=dst, send_sem=send, recv_sem=recv,
            device_id=where, device_id_type=MESH,
        )

    barrier = pltpu.get_barrier_semaphore()

    def greet(**where):
        pl.semaphore_signal(barrier, inc=1, device_id=where, device_id_type=MESH)

    for k in range(1, size):
        greet(seq=lax.rem(s + k, size))
        greet(head=lax.rem(h + k, size))
    pl.semaphore_wait(barrier, 2 * (size - 1))

    mate = lax.rem(h - s + size, size)
    apart = jnp.maximum(mate - s, s - mate)

    def tail_copies():
        behind = pl.ds(height - TAIL, TAIL)
        return (
            copy(x_ref.at[behind], x_tail, tl_send.at[0], tl_recv.at[0], seq=s + 1),
            copy(bc_ref.at[behind], bc_tail, tl_send.at[1], tl_recv.at[1], seq=s + 1),
        )

    @pl.when(s < last)
    def _():
        for each in tail_copies():
            each.start()

    @pl.when(s == 0)
    def _():
        x_tail[...] = jnp.zeros_like(x_tail)
        bc_tail[...] = jnp.zeros_like(bc_tail)
        state_in[...] = jnp.zeros_like(state_in)

    lower = lax.broadcasted_iota(jnp.int32, (height, height), 0) >= lax.broadcasted_iota(
        jnp.int32, (height, height), 1
    )
    raw = dt_ref[...] + bias_ref[...]
    steps = jnp.maximum(raw, 0.0) + jnp.log1p(jnp.exp(-jnp.abs(raw)))
    running = jnp.dot(
        jnp.where(lower, 1.0, 0.0), -jnp.exp(log_ref[...]) * steps,
        precision=lax.Precision.HIGHEST, preferred_element_type=jnp.float32,
    )
    until = jnp.exp(running[height - 1 : height] - running) * steps
    skip = jnp.broadcast_to(skip_ref[...], (height, heads))
    turned = jnp.concatenate([running, steps, until, until], axis=1).T
    table = jnp.concatenate([running, skip, until, jnp.exp(running)], axis=1)
    for j in range(chunks):
        low = j * CHUNK_HEADS
        rows[j, :CHUNK_HEADS] = turned[low : low + CHUNK_HEADS]
        rows[j, CHUNK_HEADS:] = turned[heads + low : heads + low + CHUNK_HEADS]
        cols[j] = table if j == 0 else pltpu.roll(table, 4 * heads - low, 1)

    @pl.when(s > 0)
    def _():
        for each in tail_copies():
            each.wait_recv()

    for g in range(groups):
        span = slice(g * 2 * N, (g + 1) * 2 * N)
        bc = conv_silu(joined, bc_tail[:, span], bc_ref[:, span], cbc_ref[:, span])
        b_mat, c_mat = bc[:, :N], bc[:, N:]
        c_mats[g] = c_mat
        b_turned[g] = b_mat.astype(jnp.float32).T.astype(jnp.bfloat16)
        scores[g] = lax.dot_general(
            c_mat, b_mat, (((1,), (1,)), ((), ())), preferred_element_type=jnp.float32
        )

    def state_copy(j):
        return copy(state_out.at[j], state_in.at[j], st_send.at[j], st_recv.at[j], seq=s + 1)

    def up_copy(d, j):
        place = tokens.at[s - d, j]
        return copy(place, place, up_send.at[d, j], up_recv.at[d, j], seq=s + 1)

    def up_landed(d, j):
        place = tokens.at[s - d, j]
        return copy(place, place, up_send.at[d - 1, j], up_recv.at[d - 1, j], seq=s + 1)

    def down_copy(d, j):
        place = tokens.at[s + d, j]
        return copy(place, place, dn_send.at[d, j], dn_recv.at[d, j], seq=s - 1)

    def down_landed(d, j):
        place = tokens.at[s + d, j]
        return copy(place, place, dn_send.at[d - 1, j], dn_recv.at[d - 1, j], seq=s - 1)

    sums_out[...] = jnp.zeros_like(sums_out)

    @pl.loop(0, chunks)
    def _(j):
        g = j // (chunks // groups)
        span = pl.ds(pl.multiple_of(j * wide, wide), wide)
        x = conv_silu(joined, x_tail[:, span], x_ref[:, span], cx_ref[:, span])
        x_wide = x.astype(jnp.float32)
        head_of = lax.broadcasted_iota(jnp.int32, (height, wide), 1) // P_SIZE
        col = cols[j]
        row = rows[j]

        def spread_heads(first):
            value = jnp.broadcast_to(col[:, first : first + 1], (height, wide))
            for k in range(1, CHUNK_HEADS):
                value = jnp.where(head_of == k, col[:, first + k : first + k + 1], value)
            return value

        since = spread_heads(3 * heads)
        fresh = jnp.dot(
            b_turned[g], (x_wide * spread_heads(2 * heads)).astype(jnp.bfloat16),
            preferred_element_type=jnp.float32,
        )

        @pl.when(s == 0)
        def _():
            state_out[j] = fresh.astype(jnp.bfloat16)
            state_copy(j).start()

        mixed = spread_heads(heads) * x_wide
        for k in range(CHUNK_HEADS):
            spread = jnp.where(lower, col[:, k : k + 1] - row[k : k + 1], -jnp.inf)
            mixing = scores[g] * jnp.exp(spread) * row[CHUNK_HEADS + k : CHUNK_HEADS + k + 1]
            mixed = mixed + jnp.dot(
                mixing.astype(jnp.bfloat16),
                jnp.where(head_of == k, x_wide, 0.0).astype(jnp.bfloat16),
                preferred_element_type=jnp.float32,
            )

        @pl.when(s > 0)
        def _():
            state_copy(j).wait_recv()

            @pl.when(s < last)
            def _():
                state_out[j] = (
                    fresh + since[height - 1 : height] * state_in[j].astype(jnp.float32)
                ).astype(jnp.bfloat16)
                state_copy(j).start()

        across = jnp.dot(c_mats[g], state_in[j], preferred_element_type=jnp.float32)
        gated = (mixed + since * across) * silu(z_ref[:, span].astype(jnp.float32))
        tokens[s, j] = (gated * gain_ref[:, span]).astype(jnp.bfloat16)

        @pl.when(s > 0)
        def _():
            down_copy(0, j).start()

        squares = gated * gated
        for k in range(wide // 128):
            sums_out[...] += jnp.sum(
                squares[:, k * 128 : (k + 1) * 128].T, axis=0, keepdims=True
            )

    @pl.when(s < last)
    def _():
        @pl.loop(0, chunks)
        def _(j):
            up_copy(0, j).start()

    def sums_copy(k):
        return copy(
            sums_out, sums_in.at[k - 1], ss_send.at[k - 1], ss_recv.at[k - 1],
            head=lax.rem(h + k, size),
        )

    for k in range(1, size):
        sums_copy(k).start()

    def partial_copy(t, r):
        adder = lax.rem(t + s, size)
        slot = lax.rem(h - adder + size, size) - 1
        return copy(
            partial.at[t, r], arrived.at[slot, r], rs_send.at[t, r], rs_recv.at[slot, r],
            head=adder,
        )

    def multiply(t, j):
        below = pl.ds(pl.multiple_of(j * wide, wide), wide)
        above = pl.ds(pl.multiple_of((j + 1) * wide, wide), wide)
        for n in range(0, columns, 256):
            span = slice(n, n + 256)
            value = jnp.dot(
                tokens[t, j], w_ref[below, span], preferred_element_type=jnp.float32
            ) + jnp.dot(
                tokens[t, j + 1], w_ref[above, span], preferred_element_type=jnp.float32
            )

            @pl.when(j == 0)
            def _():
                total[t, :, span] = value

            @pl.when(j > 0)
            def _():
                total[t, :, span] += value

    def hand_over(t):
        @pl.when(mate != t)
        def _():
            @pl.loop(0, parts)
            def _(r):
                piece = pl.ds(pl.multiple_of(r * some, some), some)
                partial[t, r] = total[t, piece].astype(jnp.bfloat16)
                partial_copy(t, r).start()

    @pl.loop(0, chunks // 2)
    def _(i):
        multiply(s, 2 * i)

    hand_over(s)

    sums = sums_out[...]
    for k in range(1, size):
        sums_copy(k).wait_recv()
        sums = sums + sums_in[k - 1]
    scale_out[...] = lax.rsqrt(sums / channels + epsilon)

    def scale_copy():
        return copy(scale_out, scale_in, sc_send, sc_recv, seq=mate)

    @pl.when(s != mate)
    def _():
        scale_copy().start()

    @pl.when(s == mate)
    def _():
        scale_in[...] = scale_out[...]

    def along_copy(r):
        return copy(final.at[r], passing.at[r], al_send.at[r], al_recv.at[r], seq=mate)

    def across_copy(r):
        place = out_ref.at[pl.ds(r * some, some)]
        return copy(passing.at[r], place, pm_send.at[r], pm_recv.at[r], head=mate)

    def collect():
        @pl.when(s != mate)
        def _():
            scale_copy().wait()

        scale_cols[...] = jnp.broadcast_to(scale_in[0:1], (128, height)).T

        @pl.loop(0, parts)
        def _(r):
            piece = pl.ds(pl.multiple_of(r * some, some), some)
            for k in range(1, size):
                copy(
                    partial.at[0, r], arrived.at[k - 1, r], rs_send.at[0, r],
                    rs_recv.at[k - 1, r], head=lax.rem(h + k, size),
                ).wait_recv()
            for n in range(0, columns, 128):
                span = slice(n, n + 128)
                value = total[mate, piece, span]
                for k in range(1, size):
                    value = value + arrived[k - 1, r, :, span].astype(jnp.float32)
                final[r, :, span] = (value * scale_cols[piece, :]).astype(jnp.bfloat16)

            @pl.when(s != mate)
            def _():
                along_copy(r).start()

            @pl.when(s == mate)
            def _():
                passing[r] = final[r]

    def deliver():
        @pl.loop(0, parts)
        def _(r):
            @pl.when(s != mate)
            def _():
                along_copy(r).wait_recv()

            @pl.when(s > 0)
            def _():
                across_copy(r).start()

            @pl.when(s == 0)
            def _():
                out_ref[pl.ds(pl.multiple_of(r * some, some), some)] = passing[r]

    for d in range(1, size):
        @pl.loop(0, chunks // 2)
        def _(i):
            for j in (2 * i, 2 * i + 1):
                @pl.when(s - d >= 0)
                def _():
                    up_landed(d, j).wait_recv()
                    if d < last:
                        @pl.when(s < last)
                        def _():
                            up_copy(d, j).start()

                @pl.when(s + d <= last)
                def _():
                    down_landed(d, j).wait_recv()
                    if d < last:
                        @pl.when(s > 0)
                        def _():
                            down_copy(d, j).start()

            @pl.when(s - d >= 0)
            def _():
                multiply(s - d, 2 * i)

            @pl.when(s + d <= last)
            def _():
                multiply(s + d, 2 * i)

        @pl.when(s - d >= 0)
        def _():
            hand_over(s - d)

        @pl.when(s + d <= last)
        def _():
            hand_over(s + d)

        @pl.when(apart == d - 1)
        def _():
            collect()

        if d > 1:
            @pl.when(apart == d - 2)
            def _():
                deliver()

    @pl.when(apart == last)
    def _():
        collect()

    @pl.when(apart >= last - 1)
    def _():
        deliver()

    @pl.loop(0, parts)
    def _(r):
        @pl.when(s != mate)
        def _():
            along_copy(r).wait_send()

        @pl.when(s > 0)
        def _():
            across_copy(r).wait()

    @pl.when(s < last)
    def _():
        for each in tail_copies():
            each.wait_send()

        @pl.loop(0, chunks)
        def _(j):
            state_copy(j).wait_send()

    for k in range(1, size):
        sums_copy(k).wait_send()

    for t in range(size):
        @pl.when(mate != t)
        def _():
            @pl.loop(0, parts)
            def _(r):
                partial_copy(t, r).wait_send()

    for d in range(last):
        @pl.when((s < last) & (s - d >= 0))
        def _():
            @pl.loop(0, chunks)
            def _(j):
                up_copy(d, j).wait_send()

        @pl.when((s > 0) & (s + d <= last))
        def _():
            @pl.loop(0, chunks)
            def _(j):
                down_copy(d, j).wait_send()


def square_shards(
    x_in, bc_in, z_in, dt_raw, dt_bias, a_log, d_skip, conv_x, conv_bc, norm_gain, out_weight
):
    size = lax.axis_size("seq")
    height, width = x_in.shape
    heads = dt_raw.shape[1]
    groups = bc_in.shape[1] // (2 * N)
    chunks = heads // CHUNK_HEADS
    wide = CHUNK_HEADS * P_SIZE
    columns = out_weight.shape[1]
    parts = 4
    some = height // parts
    narrow = jnp.bfloat16
    dma = pltpu.SemaphoreType.DMA
    operands = (
        x_in, bc_in, z_in, dt_raw, dt_bias[None, :], a_log[None, :], d_skip[None, :],
        conv_x, conv_bc, norm_gain[None, :], out_weight,
    )
    return pl.pallas_call(
        lambda *refs: layer_kernel(size, H * P_SIZE, *refs),
        out_shape=jax.ShapeDtypeStruct((height, columns), narrow),
        in_specs=[pl.BlockSpec(memory_space=pltpu.VMEM)] * len(operands),
        out_specs=pl.BlockSpec(memory_space=pltpu.VMEM),
        scratch_shapes=[
            pltpu.VMEM((TAIL, width), narrow),
            pltpu.VMEM((TAIL, groups * 2 * N), narrow),
            pltpu.VMEM((TAIL + height, wide), jnp.float32),
            pltpu.VMEM((chunks, height, 4 * heads), jnp.float32),
            pltpu.VMEM((chunks, 2 * CHUNK_HEADS, height), jnp.float32),
            pltpu.VMEM((groups, height, height), jnp.float32),
            pltpu.VMEM((groups, N, height), narrow),
            pltpu.VMEM((groups, height, N), narrow),
            pltpu.VMEM((chunks, N, wide), narrow),
            pltpu.VMEM((chunks, N, wide), narrow),
            pltpu.VMEM((8, height), jnp.float32),
            pltpu.VMEM((size - 1, 8, height), jnp.float32),
            pltpu.VMEM((8, height), jnp.float32),
            pltpu.VMEM((8, height), jnp.float32),
            pltpu.VMEM((size, chunks, height, wide), narrow),
            pltpu.VMEM((size, height, columns), jnp.float32),
            pltpu.VMEM((size, parts, some, columns), narrow),
            pltpu.VMEM((size - 1, parts, some, columns), narrow),
            pltpu.VMEM((parts, some, columns), narrow),
            pltpu.VMEM((parts, some, columns), narrow),
            pltpu.VMEM((height, 128), jnp.float32),
            dma((2,)), dma((2,)),
            dma((chunks,)), dma((chunks,)),
            dma((size - 1,)), dma((size - 1,)),
            dma, dma,
            dma((size - 1, chunks)), dma((size - 1, chunks)),
            dma((size - 1, chunks)), dma((size - 1, chunks)),
            dma((size, parts)), dma((size - 1, parts)),
            dma((parts,)), dma((parts,)),
            dma((parts,)), dma((parts,)),
        ],
        compiler_params=pltpu.CompilerParams(
            collective_id=0, has_side_effects=True, vmem_limit_bytes=52 * 1024 * 1024
        ),
        cost_estimate=pl.CostEstimate(
            flops=2 * size * height * width * columns, bytes_accessed=9 * height * width,
            transcendentals=heads * height * height,
        ),
        name="layer",
    )(*operands)


def from_behind(block, axis, distance):
    devices = range(lax.axis_size(axis))
    route = [(i - distance, i) for i in devices if i - distance in devices]
    return lax.ppermute(block, axis, route)


def conv_with(before, current, weight):
    height = current.shape[0]
    joined = jnp.concatenate([before, current], axis=0).astype(jnp.float32)
    summed = jnp.zeros(current.shape, jnp.float32)
    for offset in range(CONV):
        summed = summed + weight[offset][None, :] * joined[offset : offset + height]
    return summed


def shards(
    x_in, bc_in, z_in, dt_raw, dt_bias, a_log, d_skip, conv_x, conv_bc, norm_gain, out_weight
):
    height = x_in.shape[0]
    heads = dt_raw.shape[1]
    local_width = x_in.shape[1]
    nearby_groups = bc_in.shape[1] // (2 * N)
    per_group = heads // nearby_groups
    tails = from_behind((x_in[height - (CONV - 1) :], bc_in[height - (CONV - 1) :]), "seq", 1)
    input_convolved = jax.nn.silu(conv_with(tails[0], x_in, conv_x)).astype(jnp.bfloat16)
    bc_conv = jax.nn.silu(conv_with(tails[1], bc_in, conv_bc)).astype(jnp.bfloat16)
    step_sizes = jax.nn.softplus(dt_raw + dt_bias[None, :])
    log_decay = -jnp.exp(a_log)[None, :] * step_sizes
    blocks = height // BLOCK
    x_blocks = input_convolved.reshape(blocks, BLOCK, heads, P_SIZE)
    bc_blocks = bc_conv.reshape(blocks, BLOCK, nearby_groups, 2, N)
    b_mat = bc_blocks[:, :, :, 0]
    c_mat = bc_blocks[:, :, :, 1]
    running = jnp.cumsum(log_decay.reshape(blocks, BLOCK, heads), axis=1)
    step_blocks = step_sizes.reshape(blocks, BLOCK, heads)
    places = jnp.arange(BLOCK, dtype=jnp.int32)
    lower = places[:, None] >= places[None, :]

    def inside(input_rows):
        x_here, b_here, c_here, run_here, step_here = input_rows
        scores = jnp.einsum("ign,jgn->gij", c_here, b_here, preferred_element_type=jnp.float32)
        run_heads = run_here.T.reshape(nearby_groups, per_group, BLOCK)
        step_heads = step_here.T.reshape(nearby_groups, per_group, BLOCK)
        spread = run_heads[:, :, :, None] - run_heads[:, :, None, :]
        spread = jnp.where(lower[None, None], spread, -jnp.inf)
        mixing = (scores[:, None] * jnp.exp(spread) * step_heads[:, :, None, :]).astype(
            jnp.bfloat16
        )
        mixing = mixing.reshape(heads, BLOCK, BLOCK)
        within = jnp.einsum("hij,jhp->ihp", mixing, x_here, preferred_element_type=jnp.float32)
        until_finish = jnp.exp(run_here[-1:] - run_here) * step_here
        b_heads = jnp.repeat(b_here.astype(jnp.float32), per_group, axis=1)
        weighted_b = (b_heads * until_finish[:, :, None]).astype(jnp.bfloat16)
        fresh = jnp.einsum("jhn,jhp->hnp", weighted_b, x_here, preferred_element_type=jnp.float32)
        return (within, fresh)

    within, fresh = lax.map(inside, (x_blocks, b_mat, c_mat, running, step_blocks))
    since_beginning = (
        jnp.repeat(c_mat.astype(jnp.float32), per_group, axis=2) * jnp.exp(running)[..., None]
    )
    block_decay = running[:, -1, :]
    state = jnp.zeros((heads, N, P_SIZE), jnp.float32)
    prefix = jnp.zeros((heads,), jnp.float32)
    starts = [state]
    offsets = [prefix]
    state = jnp.exp(block_decay[0])[:, None, None] * state + fresh[0]
    prefix = block_decay[0]
    start_states = jnp.stack(starts)
    start_logs = jnp.stack(offsets)
    totals = lax.all_gather(prefix[None, :], "seq", axis=0, tiled=True)
    ends = jnp.cumsum(totals, axis=0)
    before = jnp.concatenate([jnp.zeros((1, heads), jnp.float32), ends[:-1]], axis=0)
    own_index = lax.axis_index("seq")
    own_before = lax.dynamic_index_in_dim(before, own_index, 0, keepdims=False)
    piece = lax.all_gather(state[None], "seq", axis=0, tiled=True)
    quantity = piece.shape[0]
    reference_point = jnp.arange(quantity, dtype=jnp.int32)
    exponent = jnp.where(
        (reference_point < own_index)[:, None], own_before[None, :] - ends, -jnp.inf
    )
    incoming = jnp.einsum("kh,khnp->hnp", jnp.exp(exponent), piece, precision=lax.Precision.HIGHEST)
    full_starts = start_states + jnp.exp(start_logs)[:, :, None, None] * incoming[None]
    across = jnp.einsum(
        "cihn,chnp->cihp", since_beginning, full_starts, precision=lax.Precision.HIGHEST
    )
    mixed = within + across + d_skip[None, None, :, None] * x_blocks.astype(jnp.float32)
    mixed = mixed.reshape(height, local_width)
    gated = mixed * jax.nn.silu(z_in.astype(jnp.float32))
    square_sums = lax.psum(jnp.sum(gated * gated, axis=1), "head")
    normed = (
        gated * lax.rsqrt(square_sums / (H * P_SIZE) + epsilon)[:, None] * norm_gain[None, :]
    ).astype(jnp.bfloat16)
    terms = jnp.dot(
        normed,
        lax.all_gather(out_weight, "seq", axis=1, tiled=True),
        preferred_element_type=jnp.float32,
    )
    return lax.psum_scatter(terms, "head", scatter_dimension=1, tiled=True).astype(jnp.bfloat16)


def solution(mesh):
    placed = (
        P(("dp", "seq"), "head"),
        P(("dp", "seq"), "head"),
        P(("dp", "seq"), "head"),
        P(("dp", "seq"), "head"),
        P("head"),
        P("head"),
        P("head"),
        P(None, "head"),
        P(None, "head"),
        P("head"),
        P("head", "seq"),
    )
    square = (
        mesh.shape["seq"] == mesh.shape["head"]
        and mesh.shape["seq"] > 1
    )
    return jax.shard_map(
        square_shards if square else shards, mesh=mesh, in_specs=placed, out_specs=P(("dp", "seq"), "head"), check_vma=False
    )
```

```python
import jax
import jax.numpy as jnp
from jax import lax
from jax.experimental import pallas as pl
from jax.experimental.pallas import tpu as pltpu
from jax.sharding import PartitionSpec as P

H = 128
P_SIZE = 64
N = 128
BLOCK = 256
CONV = 4
CHUNK_HEADS = 4
TAIL = 16
MESH = pl.DeviceIdType.MESH


epsilon = 1e-05


def silu(v):
    return v / (1.0 + jnp.exp(-v))


def conv_silu(joined, tail, current, weight):
    height = current.shape[0]
    joined[:TAIL] = tail.astype(jnp.float32)
    joined[TAIL:] = current.astype(jnp.float32)
    summed = weight[0:1] * joined[pl.ds(TAIL - CONV + 1, height)]
    for offset in range(1, CONV):
        summed = summed + weight[offset : offset + 1] * joined[
            pl.ds(TAIL - CONV + 1 + offset, height)
        ]
    return silu(summed).astype(jnp.bfloat16)


def layer_kernel(
    size, channels,
    x_ref, bc_ref, z_ref, dt_ref, bias_ref, log_ref, skip_ref, cx_ref, cbc_ref, gain_ref, w_ref,
    out_ref,
    x_tail, bc_tail, joined, cols, rows, scores, b_turned, c_mats, state_in, state_out,
    sums_out, sums_in, scale_out, scale_in, tokens, total, partial, arrived, final, passing,
    scale_cols, given_w, given_total, given_partial, given_arrived, extra_out, extra_in,
    tl_send, tl_recv, st_send, st_recv, ss_send, ss_recv, sc_send, sc_recv,
    up_send, up_recv, dn_send, dn_recv, rs_send, rs_recv, al_send, al_recv, pm_send, pm_recv,
    gf_send, gf_recv, sw_send, sw_recv, gr_send, gr_recv, ex_send, ex_recv,
):
    s = lax.axis_index("seq")
    h = lax.axis_index("head")
    height, width = x_ref.shape
    heads = dt_ref.shape[1]
    columns = w_ref.shape[1]
    chunks, wide = tokens.shape[1], tokens.shape[3]
    groups = c_mats.shape[0]
    parts = final.shape[0]
    some = height // parts
    last = size - 1

    def copy(src, dst, send, recv, **where):
        return pltpu.make_async_remote_copy(
            src_ref=src, dst_ref=dst, send_sem=send, recv_sem=recv,
            device_id=where, device_id_type=MESH,
        )

    barrier = pltpu.get_barrier_semaphore()

    def greet(**where):
        pl.semaphore_signal(barrier, inc=1, device_id=where, device_id_type=MESH)

    for k in range(1, size):
        greet(seq=lax.rem(s + k, size))
        greet(head=lax.rem(h + k, size))
    core = lax.axis_index("dp")
    greet(dp=1 - core)
    pl.semaphore_wait(barrier, 2 * (size - 1) + 1)

    given = given_w.shape[0] // wide
    at_end = (s == 0) | (s == last)
    helps = (s == 1) | (s == last - 1)
    other = jnp.where(s == 0, 1, jnp.where(s == 1, 0, jnp.where(s == last, last - 1, last)))
    low_here = jnp.where(at_end, given, 0)
    low_up = jnp.where(s == last - 1, given, 0)
    low_down = jnp.where(s == 1, given, 0)
    gifts = gf_send.shape[0]
    gift_rows = given_w.shape[0] // (2 * gifts)

    def gift_place(owner, i):
        start = pl.multiple_of((owner * gifts + i) * gift_rows, gift_rows)
        return pl.ds(start, gift_rows)

    def gift_copy(i):
        place = gift_place(core, i)
        return copy(w_ref.at[place], given_w.at[place], gf_send.at[i], gf_recv.at[i], seq=other)

    def swap_copy(i):
        place = given_w.at[gift_place(core, i)]
        return copy(place, place, sw_send.at[i], sw_recv.at[i], dp=1 - core)

    def swap_landed(i):
        place = given_w.at[gift_place(1 - core, i)]
        return copy(place, place, sw_send.at[i], sw_recv.at[i], dp=1 - core)

    mate = lax.rem(h - s + size, size)
    apart = jnp.maximum(mate - s, s - mate)

    def tail_copies():
        behind = pl.ds(height - TAIL, TAIL)
        return (
            copy(x_ref.at[behind], x_tail, tl_send.at[0], tl_recv.at[0], seq=s + 1),
            copy(bc_ref.at[behind], bc_tail, tl_send.at[1], tl_recv.at[1], seq=s + 1),
        )

    @pl.when(s < last)
    def _():
        for each in tail_copies():
            each.start()

    @pl.when(s == last)
    def _():
        for i in range(gifts):
            gift_copy(i).start()

    @pl.when(s == 0)
    def _():
        x_tail[...] = jnp.zeros_like(x_tail)
        bc_tail[...] = jnp.zeros_like(bc_tail)
        state_in[...] = jnp.zeros_like(state_in)

    lower = lax.broadcasted_iota(jnp.int32, (height, height), 0) >= lax.broadcasted_iota(
        jnp.int32, (height, height), 1
    )
    raw = dt_ref[...] + bias_ref[...]
    steps = jnp.maximum(raw, 0.0) + jnp.log1p(jnp.exp(-jnp.abs(raw)))
    running = jnp.dot(
        jnp.where(lower, 1.0, 0.0), -jnp.exp(log_ref[...]) * steps,
        precision=lax.Precision.HIGHEST, preferred_element_type=jnp.float32,
    )
    until = jnp.exp(running[height - 1 : height] - running) * steps
    skip = jnp.broadcast_to(skip_ref[...], (height, heads))
    turned = jnp.concatenate([running, steps, until, until], axis=1).T
    table = jnp.concatenate([running, skip, until, jnp.exp(running)], axis=1)
    for j in range(chunks):
        low = j * CHUNK_HEADS
        rows[j, :CHUNK_HEADS] = turned[low : low + CHUNK_HEADS]
        rows[j, CHUNK_HEADS:] = turned[heads + low : heads + low + CHUNK_HEADS]
        cols[j] = table if j == 0 else pltpu.roll(table, 4 * heads - low, 1)

    @pl.when(s > 0)
    def _():
        for each in tail_copies():
            each.wait_recv()

    for g in range(groups):
        span = slice(g * 2 * N, (g + 1) * 2 * N)
        bc = conv_silu(joined, bc_tail[:, span], bc_ref[:, span], cbc_ref[:, span])
        b_mat, c_mat = bc[:, :N], bc[:, N:]
        c_mats[g] = c_mat
        b_turned[g] = b_mat.astype(jnp.float32).T.astype(jnp.bfloat16)
        scores[g] = lax.dot_general(
            c_mat, b_mat, (((1,), (1,)), ((), ())), preferred_element_type=jnp.float32
        )

    def state_copy(j):
        return copy(state_out.at[j], state_in.at[j], st_send.at[j], st_recv.at[j], seq=s + 1)

    def up_copy(d, j):
        place = tokens.at[s - d, j]
        return copy(place, place, up_send.at[d, j], up_recv.at[d, j], seq=s + 1)

    def up_landed(d, j):
        place = tokens.at[s - d, j]
        return copy(place, place, up_send.at[d - 1, j], up_recv.at[d - 1, j], seq=s + 1)

    def down_copy(d, j):
        place = tokens.at[s + d, j]
        return copy(place, place, dn_send.at[d, j], dn_recv.at[d, j], seq=s - 1)

    def down_landed(d, j):
        place = tokens.at[s + d, j]
        return copy(place, place, dn_send.at[d - 1, j], dn_recv.at[d - 1, j], seq=s - 1)

    sums_out[...] = jnp.zeros_like(sums_out)

    @pl.when(helps | (s == mate))
    def _():
        extra_in[...] = jnp.zeros_like(extra_in)

    @pl.loop(0, chunks)
    def _(j):
        g = j // (chunks // groups)
        span = pl.ds(pl.multiple_of(j * wide, wide), wide)
        x = conv_silu(joined, x_tail[:, span], x_ref[:, span], cx_ref[:, span])
        x_wide = x.astype(jnp.float32)
        head_of = lax.broadcasted_iota(jnp.int32, (height, wide), 1) // P_SIZE
        col = cols[j]
        row = rows[j]

        def spread_heads(first):
            value = jnp.broadcast_to(col[:, first : first + 1], (height, wide))
            for k in range(1, CHUNK_HEADS):
                value = jnp.where(head_of == k, col[:, first + k : first + k + 1], value)
            return value

        since = spread_heads(3 * heads)
        fresh = jnp.dot(
            b_turned[g], (x_wide * spread_heads(2 * heads)).astype(jnp.bfloat16),
            preferred_element_type=jnp.float32,
        )

        @pl.when(s == 0)
        def _():
            state_out[j] = fresh.astype(jnp.bfloat16)
            state_copy(j).start()

        mixed = spread_heads(heads) * x_wide
        for k in range(CHUNK_HEADS):
            spread = jnp.where(lower, col[:, k : k + 1] - row[k : k + 1], -jnp.inf)
            mixing = scores[g] * jnp.exp(spread) * row[CHUNK_HEADS + k : CHUNK_HEADS + k + 1]
            mixed = mixed + jnp.dot(
                mixing.astype(jnp.bfloat16),
                jnp.where(head_of == k, x_wide, 0.0).astype(jnp.bfloat16),
                preferred_element_type=jnp.float32,
            )

        @pl.when(s > 0)
        def _():
            state_copy(j).wait_recv()

            @pl.when(s < last)
            def _():
                state_out[j] = (
                    fresh + since[height - 1 : height] * state_in[j].astype(jnp.float32)
                ).astype(jnp.bfloat16)
                state_copy(j).start()

        across = jnp.dot(c_mats[g], state_in[j], preferred_element_type=jnp.float32)
        gated = (mixed + since * across) * silu(z_ref[:, span].astype(jnp.float32))
        tokens[s, j] = (gated * gain_ref[:, span]).astype(jnp.bfloat16)

        @pl.when((s > 0) & (j >= low_down))
        def _():
            down_copy(0, j).start()

        squares = gated * gated
        for k in range(wide // 128):
            sums_out[...] += jnp.sum(
                squares[:, k * 128 : (k + 1) * 128].T, axis=0, keepdims=True
            )

    @pl.when(s < last)
    def _():
        @pl.loop(low_up, chunks)
        def _(j):
            up_copy(0, j).start()

            @pl.when((s == 0) & (j >= chunks - gifts))
            def _():
                gift_copy(j - (chunks - gifts)).start()

    def sums_copy(k):
        return copy(
            sums_out, sums_in.at[k - 1], ss_send.at[k - 1], ss_recv.at[k - 1],
            head=lax.rem(h + k, size),
        )

    for k in range(1, size):
        sums_copy(k).start()

    def partial_copy(t, r):
        adder = lax.rem(t + s, size)
        slot = lax.rem(h - adder + size, size) - 1
        return copy(
            partial.at[t, r], arrived.at[slot, r], rs_send.at[t, r], rs_recv.at[slot, r],
            head=adder,
        )

    def multiply(t, j, first, weight, sums):
        below = pl.ds(pl.multiple_of(j * wide, wide), wide)
        above = pl.ds(pl.multiple_of((j + 1) * wide, wide), wide)
        for n in range(0, columns, 256):
            span = slice(n, n + 256)
            value = jnp.dot(
                tokens[t, j], weight[below, span], preferred_element_type=jnp.float32
            ) + jnp.dot(
                tokens[t, j + 1], weight[above, span], preferred_element_type=jnp.float32
            )

            @pl.when(j == first)
            def _():
                sums[t, :, span] = value

            @pl.when(j > first)
            def _():
                sums[t, :, span] += value

    def given_copy(t, r):
        adder = lax.rem(t + other, size)
        slot = lax.rem(h - adder + size, size) - 1
        return copy(
            given_partial.at[t, r], given_arrived.at[slot, r], gr_send.at[t, r],
            gr_recv.at[slot, r], head=adder,
        )

    given_mate = lax.rem(h - other + size, size)

    def multiply_given(t):
        @pl.loop(0, given // 2)
        def _(i):
            multiply(t, 2 * i, 0, given_w, given_total)

        @pl.when(given_mate != t)
        def _():
            @pl.loop(0, parts)
            def _(r):
                piece = pl.ds(pl.multiple_of(r * some, some), some)
                given_partial[t, r] = given_total[t, piece].astype(jnp.bfloat16)
                given_copy(t, r).start()

    def extra_copy(r):
        return copy(extra_out.at[r], extra_in.at[r], ex_send.at[r], ex_recv.at[r], seq=other)

    def collect_given():
        @pl.loop(0, parts)
        def _(r):
            piece = pl.ds(pl.multiple_of(r * some, some), some)
            for k in range(1, size):
                copy(
                    given_partial.at[0, r], given_arrived.at[k - 1, r], gr_send.at[0, r],
                    gr_recv.at[k - 1, r], head=lax.rem(h + k, size),
                ).wait_recv()
            for n in range(0, columns, 128):
                span = slice(n, n + 128)
                value = given_total[given_mate, piece, span]
                for k in range(1, size):
                    value = value + given_arrived[k - 1, r, :, span].astype(jnp.float32)
                extra_out[r, :, span] = value.astype(jnp.bfloat16)
            extra_copy(r).start()

    def hand_over(t):
        @pl.when(mate != t)
        def _():
            @pl.loop(0, parts)
            def _(r):
                piece = pl.ds(pl.multiple_of(r * some, some), some)
                partial[t, r] = total[t, piece].astype(jnp.bfloat16)
                partial_copy(t, r).start()

    @pl.loop(0, chunks // 2)
    def _(i):
        multiply(s, 2 * i, 0, w_ref, total)

    hand_over(s)

    sums = sums_out[...]
    for k in range(1, size):
        sums_copy(k).wait_recv()
        sums = sums + sums_in[k - 1]
    scale_out[...] = lax.rsqrt(sums / channels + epsilon)

    def scale_copy():
        return copy(scale_out, scale_in, sc_send, sc_recv, seq=mate)

    @pl.when(s != mate)
    def _():
        scale_copy().start()

    @pl.when(s == mate)
    def _():
        scale_in[...] = scale_out[...]

    def along_copy(r):
        return copy(final.at[r], passing.at[r], al_send.at[r], al_recv.at[r], seq=mate)

    def across_copy(r):
        place = out_ref.at[pl.ds(r * some, some)]
        return copy(passing.at[r], place, pm_send.at[r], pm_recv.at[r], head=mate)

    with_extra = at_end & (s != mate)

    def collect():
        @pl.when(s != mate)
        def _():
            scale_copy().wait()

        scale_cols[...] = jnp.broadcast_to(scale_in[0:1], (128, height)).T

        @pl.loop(0, parts)
        def _(r):
            piece = pl.ds(pl.multiple_of(r * some, some), some)
            for k in range(1, size):
                copy(
                    partial.at[0, r], arrived.at[k - 1, r], rs_send.at[0, r],
                    rs_recv.at[k - 1, r], head=lax.rem(h + k, size),
                ).wait_recv()

            @pl.when(with_extra)
            def _():
                extra_copy(r).wait_recv()

            for n in range(0, columns, 128):
                span = slice(n, n + 128)
                value = total[mate, piece, span]
                for k in range(1, size):
                    value = value + arrived[k - 1, r, :, span].astype(jnp.float32)
                value = value + extra_in[r, :, span].astype(jnp.float32)
                final[r, :, span] = (value * scale_cols[piece, :]).astype(jnp.bfloat16)

            @pl.when(s != mate)
            def _():
                along_copy(r).start()

            @pl.when(s == mate)
            def _():
                passing[r] = final[r]

    def deliver():
        @pl.loop(0, parts)
        def _(r):
            @pl.when(s != mate)
            def _():
                along_copy(r).wait_recv()

            @pl.when(s > 0)
            def _():
                across_copy(r).start()

            @pl.when(s == 0)
            def _():
                out_ref[pl.ds(pl.multiple_of(r * some, some), some)] = passing[r]

    for d in range(1, size):
        @pl.loop(low_here // 2, chunks // 2)
        def _(i):
            for j in (2 * i, 2 * i + 1):
                @pl.when(s - d >= 0)
                def _():
                    up_landed(d, j).wait_recv()
                    if d < last:
                        @pl.when((s < last) & (j >= low_up))
                        def _():
                            up_copy(d, j).start()

                @pl.when(s + d <= last)
                def _():
                    down_landed(d, j).wait_recv()
                    if d < last:
                        @pl.when((s > 0) & (j >= low_down))
                        def _():
                            down_copy(d, j).start()

            @pl.when(s - d >= 0)
            def _():
                multiply(s - d, 2 * i, low_here, w_ref, total)

            @pl.when(s + d <= last)
            def _():
                multiply(s + d, 2 * i, low_here, w_ref, total)

        @pl.when(s - d >= 0)
        def _():
            hand_over(s - d)

        @pl.when(s + d <= last)
        def _():
            hand_over(s + d)

        if d == 1:
            @pl.when(helps)
            def _():
                for i in range(gifts):
                    gift_copy(i).wait_recv()
                    swap_copy(i).start()
                for i in range(gifts):
                    swap_landed(i).wait_recv()
                multiply_given(s)
                multiply_given(last - s)

        if d == 2:
            @pl.when(helps)
            def _():
                multiply_given(last - other)

                @pl.when(given_mate != other)
                def _():
                    collect_given()

        @pl.when((apart == d - 1) & (helps | (s == mate)))
        def _():
            collect()

        if d > 1:
            @pl.when((apart == d - 2) & ~with_extra)
            def _():
                deliver()

    @pl.when((apart == last) | with_extra)
    def _():
        collect()

    @pl.when((apart >= last - 1) | with_extra)
    def _():
        deliver()

    @pl.when(at_end)
    def _():
        for i in range(gifts):
            gift_copy(i).wait_send()

    @pl.when(helps)
    def _():
        for i in range(gifts):
            swap_copy(i).wait_send()
        for t in range(size):
            @pl.when((given_mate != t) & (other != t))
            def _():
                @pl.loop(0, parts)
                def _(r):
                    given_copy(t, r).wait_send()

        @pl.when(given_mate != other)
        def _():
            @pl.loop(0, parts)
            def _(r):
                extra_copy(r).wait_send()

    @pl.loop(0, parts)
    def _(r):
        @pl.when(s != mate)
        def _():
            along_copy(r).wait_send()

        @pl.when(s > 0)
        def _():
            across_copy(r).wait()

    @pl.when(s < last)
    def _():
        for each in tail_copies():
            each.wait_send()

        @pl.loop(0, chunks)
        def _(j):
            state_copy(j).wait_send()

    for k in range(1, size):
        sums_copy(k).wait_send()

    for t in range(size):
        @pl.when(mate != t)
        def _():
            @pl.loop(0, parts)
            def _(r):
                partial_copy(t, r).wait_send()

    for d in range(last):
        @pl.when((s < last) & (s - d >= 0))
        def _():
            @pl.loop(low_up, chunks)
            def _(j):
                up_copy(d, j).wait_send()

        @pl.when((s > 0) & (s + d <= last))
        def _():
            @pl.loop(low_down, chunks)
            def _(j):
                down_copy(d, j).wait_send()


def square_shards(
    x_in, bc_in, z_in, dt_raw, dt_bias, a_log, d_skip, conv_x, conv_bc, norm_gain, out_weight
):
    size = lax.axis_size("seq")
    height, width = x_in.shape
    heads = dt_raw.shape[1]
    groups = bc_in.shape[1] // (2 * N)
    chunks = heads // CHUNK_HEADS
    wide = CHUNK_HEADS * P_SIZE
    columns = out_weight.shape[1]
    parts = 4
    given = chunks // 2
    gifts = 4
    some = height // parts
    narrow = jnp.bfloat16
    dma = pltpu.SemaphoreType.DMA
    operands = (
        x_in, bc_in, z_in, dt_raw, dt_bias[None, :], a_log[None, :], d_skip[None, :],
        conv_x, conv_bc, norm_gain[None, :], out_weight,
    )
    return pl.pallas_call(
        lambda *refs: layer_kernel(size, H * P_SIZE, *refs),
        out_shape=jax.ShapeDtypeStruct((height, columns), narrow),
        in_specs=[pl.BlockSpec(memory_space=pltpu.VMEM)] * len(operands),
        out_specs=pl.BlockSpec(memory_space=pltpu.VMEM),
        scratch_shapes=[
            pltpu.VMEM((TAIL, width), narrow),
            pltpu.VMEM((TAIL, groups * 2 * N), narrow),
            pltpu.VMEM((TAIL + height, wide), jnp.float32),
            pltpu.VMEM((chunks, height, 4 * heads), jnp.float32),
            pltpu.VMEM((chunks, 2 * CHUNK_HEADS, height), jnp.float32),
            pltpu.VMEM((groups, height, height), jnp.float32),
            pltpu.VMEM((groups, N, height), narrow),
            pltpu.VMEM((groups, height, N), narrow),
            pltpu.VMEM((chunks, N, wide), narrow),
            pltpu.VMEM((chunks, N, wide), narrow),
            pltpu.VMEM((8, height), jnp.float32),
            pltpu.VMEM((size - 1, 8, height), jnp.float32),
            pltpu.VMEM((8, height), jnp.float32),
            pltpu.VMEM((8, height), jnp.float32),
            pltpu.VMEM((size, chunks, height, wide), narrow),
            pltpu.VMEM((size, height, columns), jnp.float32),
            pltpu.VMEM((size, parts, some, columns), narrow),
            pltpu.VMEM((size - 1, parts, some, columns), narrow),
            pltpu.VMEM((parts, some, columns), narrow),
            pltpu.VMEM((parts, some, columns), narrow),
            pltpu.VMEM((height, 128), jnp.float32),
            pltpu.VMEM((given * wide, columns), narrow),
            pltpu.VMEM((size, height, columns), jnp.float32),
            pltpu.VMEM((size, parts, some, columns), narrow),
            pltpu.VMEM((size - 1, parts, some, columns), narrow),
            pltpu.VMEM((parts, some, columns), narrow),
            pltpu.VMEM((parts, some, columns), narrow),
            dma((2,)), dma((2,)),
            dma((chunks,)), dma((chunks,)),
            dma((size - 1,)), dma((size - 1,)),
            dma, dma,
            dma((size - 1, chunks)), dma((size - 1, chunks)),
            dma((size - 1, chunks)), dma((size - 1, chunks)),
            dma((size, parts)), dma((size - 1, parts)),
            dma((parts,)), dma((parts,)),
            dma((parts,)), dma((parts,)),
            dma((gifts,)), dma((gifts,)),
            dma((gifts,)), dma((gifts,)),
            dma((size, parts)), dma((size - 1, parts)),
            dma((parts,)), dma((parts,)),
        ],
        compiler_params=pltpu.CompilerParams(
            collective_id=0, has_side_effects=True, vmem_limit_bytes=52 * 1024 * 1024
        ),
        cost_estimate=pl.CostEstimate(
            flops=2 * size * height * width * columns, bytes_accessed=9 * height * width,
            transcendentals=heads * height * height,
        ),
        name="layer",
    )(*operands)


def from_behind(block, axis, distance):
    devices = range(lax.axis_size(axis))
    route = [(i - distance, i) for i in devices if i - distance in devices]
    return lax.ppermute(block, axis, route)


def conv_with(before, current, weight):
    height = current.shape[0]
    joined = jnp.concatenate([before, current], axis=0).astype(jnp.float32)
    summed = jnp.zeros(current.shape, jnp.float32)
    for offset in range(CONV):
        summed = summed + weight[offset][None, :] * joined[offset : offset + height]
    return summed


def shards(
    x_in, bc_in, z_in, dt_raw, dt_bias, a_log, d_skip, conv_x, conv_bc, norm_gain, out_weight
):
    height = x_in.shape[0]
    heads = dt_raw.shape[1]
    local_width = x_in.shape[1]
    nearby_groups = bc_in.shape[1] // (2 * N)
    per_group = heads // nearby_groups
    tails = from_behind((x_in[height - (CONV - 1) :], bc_in[height - (CONV - 1) :]), "seq", 1)
    input_convolved = jax.nn.silu(conv_with(tails[0], x_in, conv_x)).astype(jnp.bfloat16)
    bc_conv = jax.nn.silu(conv_with(tails[1], bc_in, conv_bc)).astype(jnp.bfloat16)
    step_sizes = jax.nn.softplus(dt_raw + dt_bias[None, :])
    log_decay = -jnp.exp(a_log)[None, :] * step_sizes
    blocks = height // BLOCK
    x_blocks = input_convolved.reshape(blocks, BLOCK, heads, P_SIZE)
    bc_blocks = bc_conv.reshape(blocks, BLOCK, nearby_groups, 2, N)
    b_mat = bc_blocks[:, :, :, 0]
    c_mat = bc_blocks[:, :, :, 1]
    running = jnp.cumsum(log_decay.reshape(blocks, BLOCK, heads), axis=1)
    step_blocks = step_sizes.reshape(blocks, BLOCK, heads)
    places = jnp.arange(BLOCK, dtype=jnp.int32)
    lower = places[:, None] >= places[None, :]

    def inside(input_rows):
        x_here, b_here, c_here, run_here, step_here = input_rows
        scores = jnp.einsum("ign,jgn->gij", c_here, b_here, preferred_element_type=jnp.float32)
        run_heads = run_here.T.reshape(nearby_groups, per_group, BLOCK)
        step_heads = step_here.T.reshape(nearby_groups, per_group, BLOCK)
        spread = run_heads[:, :, :, None] - run_heads[:, :, None, :]
        spread = jnp.where(lower[None, None], spread, -jnp.inf)
        mixing = (scores[:, None] * jnp.exp(spread) * step_heads[:, :, None, :]).astype(
            jnp.bfloat16
        )
        mixing = mixing.reshape(heads, BLOCK, BLOCK)
        within = jnp.einsum("hij,jhp->ihp", mixing, x_here, preferred_element_type=jnp.float32)
        until_finish = jnp.exp(run_here[-1:] - run_here) * step_here
        b_heads = jnp.repeat(b_here.astype(jnp.float32), per_group, axis=1)
        weighted_b = (b_heads * until_finish[:, :, None]).astype(jnp.bfloat16)
        fresh = jnp.einsum("jhn,jhp->hnp", weighted_b, x_here, preferred_element_type=jnp.float32)
        return (within, fresh)

    within, fresh = lax.map(inside, (x_blocks, b_mat, c_mat, running, step_blocks))
    since_beginning = (
        jnp.repeat(c_mat.astype(jnp.float32), per_group, axis=2) * jnp.exp(running)[..., None]
    )
    block_decay = running[:, -1, :]
    state = jnp.zeros((heads, N, P_SIZE), jnp.float32)
    prefix = jnp.zeros((heads,), jnp.float32)
    starts = [state]
    offsets = [prefix]
    state = jnp.exp(block_decay[0])[:, None, None] * state + fresh[0]
    prefix = block_decay[0]
    start_states = jnp.stack(starts)
    start_logs = jnp.stack(offsets)
    totals = lax.all_gather(prefix[None, :], "seq", axis=0, tiled=True)
    ends = jnp.cumsum(totals, axis=0)
    before = jnp.concatenate([jnp.zeros((1, heads), jnp.float32), ends[:-1]], axis=0)
    own_index = lax.axis_index("seq")
    own_before = lax.dynamic_index_in_dim(before, own_index, 0, keepdims=False)
    piece = lax.all_gather(state[None], "seq", axis=0, tiled=True)
    quantity = piece.shape[0]
    reference_point = jnp.arange(quantity, dtype=jnp.int32)
    exponent = jnp.where(
        (reference_point < own_index)[:, None], own_before[None, :] - ends, -jnp.inf
    )
    incoming = jnp.einsum("kh,khnp->hnp", jnp.exp(exponent), piece, precision=lax.Precision.HIGHEST)
    full_starts = start_states + jnp.exp(start_logs)[:, :, None, None] * incoming[None]
    across = jnp.einsum(
        "cihn,chnp->cihp", since_beginning, full_starts, precision=lax.Precision.HIGHEST
    )
    mixed = within + across + d_skip[None, None, :, None] * x_blocks.astype(jnp.float32)
    mixed = mixed.reshape(height, local_width)
    gated = mixed * jax.nn.silu(z_in.astype(jnp.float32))
    square_sums = lax.psum(jnp.sum(gated * gated, axis=1), "head")
    normed = (
        gated * lax.rsqrt(square_sums / (H * P_SIZE) + epsilon)[:, None] * norm_gain[None, :]
    ).astype(jnp.bfloat16)
    terms = jnp.dot(
        normed,
        lax.all_gather(out_weight, "seq", axis=1, tiled=True),
        preferred_element_type=jnp.float32,
    )
    return lax.psum_scatter(terms, "head", scatter_dimension=1, tiled=True).astype(jnp.bfloat16)


def solution(mesh):
    placed = (
        P(("dp", "seq"), "head"),
        P(("dp", "seq"), "head"),
        P(("dp", "seq"), "head"),
        P(("dp", "seq"), "head"),
        P("head"),
        P("head"),
        P("head"),
        P(None, "head"),
        P(None, "head"),
        P("head"),
        P("head", "seq"),
    )
    shape = mesh.shape
    square = shape["seq"] == 4 and shape["head"] == 4 and shape["dp"] == 2
    return jax.shard_map(
        square_shards if square else shards, mesh=mesh, in_specs=placed, out_specs=P(("dp", "seq"), "head"), check_vma=False
    )
```

```python
import jax
import jax.numpy as jnp
from jax import lax
from jax.experimental import pallas as pl
from jax.experimental.pallas import tpu as pltpu
from jax.sharding import PartitionSpec as P

H = 128
P_SIZE = 64
N = 128
BLOCK = 256
CONV = 4
CHUNK_HEADS = 4
TAIL = 16
MESH = pl.DeviceIdType.MESH


epsilon = 1e-05


def silu(v):
    return v / (1.0 + jnp.exp(-v))


def conv_silu(joined, tail, current, weight):
    height = current.shape[0]
    joined[:TAIL] = tail.astype(jnp.float32)
    joined[TAIL:] = current.astype(jnp.float32)
    summed = weight[0:1] * joined[pl.ds(TAIL - CONV + 1, height)]
    for offset in range(1, CONV):
        summed = summed + weight[offset : offset + 1] * joined[
            pl.ds(TAIL - CONV + 1 + offset, height)
        ]
    return silu(summed).astype(jnp.bfloat16)


def layer_kernel(
    size, channels,
    x_ref, bc_ref, z_ref, dt_ref, bias_ref, log_ref, skip_ref, cx_ref, cbc_ref, gain_ref, w_ref,
    out_ref,
    x_tail, bc_tail, joined, cols, rows, scores, b_turned, c_mats, state_in, state_out,
    sums_out, sums_in, scale_out, scale_in, tokens, total, partial, arrived, final, passing,
    scale_cols, given_w, given_total, given_partial, given_arrived, extra_out, extra_in,
    tl_send, tl_recv, st_send, st_recv, ss_send, ss_recv, sc_send, sc_recv,
    up_send, up_recv, dn_send, dn_recv, rs_send, rs_recv, al_send, al_recv, pm_send, pm_recv,
    gf_send, gf_recv, sw_send, sw_recv, gr_send, gr_recv, ex_send, ex_recv,
):
    s = lax.axis_index("seq")
    h = lax.axis_index("head")
    height, width = x_ref.shape
    heads = dt_ref.shape[1]
    columns = w_ref.shape[1]
    chunks, wide = tokens.shape[1], tokens.shape[3]
    groups = c_mats.shape[0]
    parts = final.shape[0]
    some = height // parts
    last = size - 1

    def copy(src, dst, send, recv, **where):
        return pltpu.make_async_remote_copy(
            src_ref=src, dst_ref=dst, send_sem=send, recv_sem=recv,
            device_id=where, device_id_type=MESH,
        )

    barrier = pltpu.get_barrier_semaphore()

    def greet(**where):
        pl.semaphore_signal(barrier, inc=1, device_id=where, device_id_type=MESH)

    for k in range(1, size):
        greet(seq=lax.rem(s + k, size))
        greet(head=lax.rem(h + k, size))
    core = lax.axis_index("dp")
    greet(dp=1 - core)
    pl.semaphore_wait(barrier, 2 * (size - 1) + 1)

    given = given_w.shape[0] // wide
    at_end = (s == 0) | (s == last)
    helps = (s == 1) | (s == last - 1)
    other = jnp.where(s == 0, 1, jnp.where(s == 1, 0, jnp.where(s == last, last - 1, last)))
    low_here = jnp.where(at_end, given, 0)
    low_up = jnp.where(s == last - 1, given, 0)
    low_down = jnp.where(s == 1, given, 0)
    gifts = gf_send.shape[0]
    gift_rows = given_w.shape[0] // (2 * gifts)

    def gift_place(owner, i):
        start = pl.multiple_of((owner * gifts + i) * gift_rows, gift_rows)
        return pl.ds(start, gift_rows)

    def gift_copy(i):
        place = gift_place(core, i)
        return copy(w_ref.at[place], given_w.at[place], gf_send.at[i], gf_recv.at[i], seq=other)

    def swap_copy(i):
        place = given_w.at[gift_place(core, i)]
        return copy(place, place, sw_send.at[i], sw_recv.at[i], dp=1 - core)

    def swap_landed(i):
        place = given_w.at[gift_place(1 - core, i)]
        return copy(place, place, sw_send.at[i], sw_recv.at[i], dp=1 - core)

    mate = lax.rem(h - s + size, size)
    apart = jnp.maximum(mate - s, s - mate)

    def tail_copies():
        behind = pl.ds(height - TAIL, TAIL)
        return (
            copy(x_ref.at[behind], x_tail, tl_send.at[0], tl_recv.at[0], seq=s + 1),
            copy(bc_ref.at[behind], bc_tail, tl_send.at[1], tl_recv.at[1], seq=s + 1),
        )

    @pl.when(s < last)
    def _():
        for each in tail_copies():
            each.start()

    @pl.when(s == last)
    def _():
        for i in range(gifts):
            gift_copy(i).start()

    @pl.when(s == 0)
    def _():
        x_tail[...] = jnp.zeros_like(x_tail)
        bc_tail[...] = jnp.zeros_like(bc_tail)
        state_in[...] = jnp.zeros_like(state_in)

    lower = lax.broadcasted_iota(jnp.int32, (height, height), 0) >= lax.broadcasted_iota(
        jnp.int32, (height, height), 1
    )
    raw = dt_ref[...] + bias_ref[...]
    steps = jnp.maximum(raw, 0.0) + jnp.log1p(jnp.exp(-jnp.abs(raw)))
    running = jnp.dot(
        jnp.where(lower, 1.0, 0.0), -jnp.exp(log_ref[...]) * steps,
        precision=lax.Precision.HIGHEST, preferred_element_type=jnp.float32,
    )
    until = jnp.exp(running[height - 1 : height] - running) * steps
    skip = jnp.broadcast_to(skip_ref[...], (height, heads))
    turned = jnp.concatenate([running, steps, until, until], axis=1).T
    table = jnp.concatenate([running, skip, until, jnp.exp(running)], axis=1)
    for j in range(chunks):
        low = j * CHUNK_HEADS
        rows[j, :CHUNK_HEADS] = turned[low : low + CHUNK_HEADS]
        rows[j, CHUNK_HEADS:] = turned[heads + low : heads + low + CHUNK_HEADS]
        cols[j] = table if j == 0 else pltpu.roll(table, 4 * heads - low, 1)

    @pl.when(s > 0)
    def _():
        for each in tail_copies():
            each.wait_recv()

    for g in range(groups):
        span = slice(g * 2 * N, (g + 1) * 2 * N)
        bc = conv_silu(joined, bc_tail[:, span], bc_ref[:, span], cbc_ref[:, span])
        b_mat, c_mat = bc[:, :N], bc[:, N:]
        c_mats[g] = c_mat
        b_turned[g] = b_mat.astype(jnp.float32).T.astype(jnp.bfloat16)
        scores[g] = lax.dot_general(
            c_mat, b_mat, (((1,), (1,)), ((), ())), preferred_element_type=jnp.float32
        )

    def state_copy(j):
        return copy(state_out.at[j], state_in.at[j], st_send.at[j], st_recv.at[j], seq=s + 1)

    def up_copy(d, j):
        place = tokens.at[s - d, j]
        return copy(place, place, up_send.at[d, j], up_recv.at[d, j], seq=s + 1)

    def up_landed(d, j):
        place = tokens.at[s - d, j]
        return copy(place, place, up_send.at[d - 1, j], up_recv.at[d - 1, j], seq=s + 1)

    def down_copy(d, j):
        place = tokens.at[s + d, j]
        return copy(place, place, dn_send.at[d, j], dn_recv.at[d, j], seq=s - 1)

    def down_landed(d, j):
        place = tokens.at[s + d, j]
        return copy(place, place, dn_send.at[d - 1, j], dn_recv.at[d - 1, j], seq=s - 1)

    sums_out[...] = jnp.zeros_like(sums_out)

    @pl.when(helps | (s == mate))
    def _():
        extra_in[...] = jnp.zeros_like(extra_in)

    @pl.loop(0, chunks)
    def _(j):
        g = j // (chunks // groups)
        span = pl.ds(pl.multiple_of(j * wide, wide), wide)
        x = conv_silu(joined, x_tail[:, span], x_ref[:, span], cx_ref[:, span])
        x_wide = x.astype(jnp.float32)
        head_of = lax.broadcasted_iota(jnp.int32, (height, wide), 1) // P_SIZE
        col = cols[j]
        row = rows[j]

        def spread_heads(first):
            value = jnp.broadcast_to(col[:, first : first + 1], (height, wide))
            for k in range(1, CHUNK_HEADS):
                value = jnp.where(head_of == k, col[:, first + k : first + k + 1], value)
            return value

        since = spread_heads(3 * heads)
        fresh = jnp.dot(
            b_turned[g], (x_wide * spread_heads(2 * heads)).astype(jnp.bfloat16),
            preferred_element_type=jnp.float32,
        )

        @pl.when(s == 0)
        def _():
            state_out[j] = fresh.astype(jnp.bfloat16)
            state_copy(j).start()

        mixed = spread_heads(heads) * x_wide
        for k in range(CHUNK_HEADS):
            spread = jnp.where(lower, col[:, k : k + 1] - row[k : k + 1], -jnp.inf)
            mixing = scores[g] * jnp.exp(spread) * row[CHUNK_HEADS + k : CHUNK_HEADS + k + 1]
            mixed = mixed + jnp.dot(
                mixing.astype(jnp.bfloat16),
                jnp.where(head_of == k, x_wide, 0.0).astype(jnp.bfloat16),
                preferred_element_type=jnp.float32,
            )

        @pl.when(s > 0)
        def _():
            state_copy(j).wait_recv()

            @pl.when(s < last)
            def _():
                state_out[j] = (
                    fresh + since[height - 1 : height] * state_in[j].astype(jnp.float32)
                ).astype(jnp.bfloat16)
                state_copy(j).start()

        across = jnp.dot(c_mats[g], state_in[j], preferred_element_type=jnp.float32)
        gated = (mixed + since * across) * silu(z_ref[:, span].astype(jnp.float32))
        tokens[s, j] = (gated * gain_ref[:, span]).astype(jnp.bfloat16)

        @pl.when((s > 0) & (j >= low_down))
        def _():
            down_copy(0, j).start()

        squares = gated * gated
        for k in range(wide // 128):
            sums_out[...] += jnp.sum(
                squares[:, k * 128 : (k + 1) * 128].T, axis=0, keepdims=True
            )

    @pl.when(s < last)
    def _():
        @pl.when(s == 0)
        def _():
            for i in range(gifts):
                gift_copy(i).start()

        @pl.loop(low_up, chunks)
        def _(j):
            up_copy(0, j).start()

    def sums_copy(k):
        return copy(
            sums_out, sums_in.at[k - 1], ss_send.at[k - 1], ss_recv.at[k - 1],
            head=lax.rem(h + k, size),
        )

    for k in range(1, size):
        sums_copy(k).start()

    def partial_copy(t, r):
        adder = lax.rem(t + s, size)
        slot = lax.rem(h - adder + size, size) - 1
        return copy(
            partial.at[t, r], arrived.at[slot, r], rs_send.at[t, r], rs_recv.at[slot, r],
            head=adder,
        )

    def multiply(t, j, first, weight, sums):
        below = pl.ds(pl.multiple_of(j * wide, wide), wide)
        above = pl.ds(pl.multiple_of((j + 1) * wide, wide), wide)
        for n in range(0, columns, 256):
            span = slice(n, n + 256)
            value = jnp.dot(
                tokens[t, j], weight[below, span], preferred_element_type=jnp.float32
            ) + jnp.dot(
                tokens[t, j + 1], weight[above, span], preferred_element_type=jnp.float32
            )

            @pl.when(j == first)
            def _():
                sums[t, :, span] = value

            @pl.when(j > first)
            def _():
                sums[t, :, span] += value

    def given_copy(t, r):
        adder = lax.rem(t + other, size)
        slot = lax.rem(h - adder + size, size) - 1
        return copy(
            given_partial.at[t, r], given_arrived.at[slot, r], gr_send.at[t, r],
            gr_recv.at[slot, r], head=adder,
        )

    given_mate = lax.rem(h - other + size, size)

    def multiply_given(t):
        @pl.loop(0, given // 2)
        def _(i):
            multiply(t, 2 * i, 0, given_w, given_total)

        @pl.when(given_mate != t)
        def _():
            @pl.loop(0, parts)
            def _(r):
                piece = pl.ds(pl.multiple_of(r * some, some), some)
                given_partial[t, r] = given_total[t, piece].astype(jnp.bfloat16)
                given_copy(t, r).start()

    def extra_copy(r):
        return copy(extra_out.at[r], extra_in.at[r], ex_send.at[r], ex_recv.at[r], seq=other)

    def collect_given():
        @pl.loop(0, parts)
        def _(r):
            piece = pl.ds(pl.multiple_of(r * some, some), some)
            for k in range(1, size):
                copy(
                    given_partial.at[0, r], given_arrived.at[k - 1, r], gr_send.at[0, r],
                    gr_recv.at[k - 1, r], head=lax.rem(h + k, size),
                ).wait_recv()
            for n in range(0, columns, 128):
                span = slice(n, n + 128)
                value = given_total[given_mate, piece, span]
                for k in range(1, size):
                    value = value + given_arrived[k - 1, r, :, span].astype(jnp.float32)
                extra_out[r, :, span] = value.astype(jnp.bfloat16)
            extra_copy(r).start()

    def hand_over(t):
        @pl.when(mate != t)
        def _():
            @pl.loop(0, parts)
            def _(r):
                piece = pl.ds(pl.multiple_of(r * some, some), some)
                partial[t, r] = total[t, piece].astype(jnp.bfloat16)
                partial_copy(t, r).start()

    @pl.loop(0, chunks // 2)
    def _(i):
        multiply(s, 2 * i, 0, w_ref, total)

    hand_over(s)

    sums = sums_out[...]
    for k in range(1, size):
        sums_copy(k).wait_recv()
        sums = sums + sums_in[k - 1]
    scale_out[...] = lax.rsqrt(sums / channels + epsilon)

    def scale_copy():
        return copy(scale_out, scale_in, sc_send, sc_recv, seq=mate)

    @pl.when(s != mate)
    def _():
        scale_copy().start()

    @pl.when(s == mate)
    def _():
        scale_in[...] = scale_out[...]

    def along_copy(r):
        return copy(final.at[r], passing.at[r], al_send.at[r], al_recv.at[r], seq=mate)

    def across_copy(r):
        place = out_ref.at[pl.ds(r * some, some)]
        return copy(passing.at[r], place, pm_send.at[r], pm_recv.at[r], head=mate)

    with_extra = at_end & (s != mate)

    def collect():
        @pl.when(s != mate)
        def _():
            scale_copy().wait()

        scale_cols[...] = jnp.broadcast_to(scale_in[0:1], (128, height)).T

        @pl.loop(0, parts)
        def _(r):
            piece = pl.ds(pl.multiple_of(r * some, some), some)
            for k in range(1, size):
                copy(
                    partial.at[0, r], arrived.at[k - 1, r], rs_send.at[0, r],
                    rs_recv.at[k - 1, r], head=lax.rem(h + k, size),
                ).wait_recv()

            @pl.when(with_extra)
            def _():
                extra_copy(r).wait_recv()

            for n in range(0, columns, 128):
                span = slice(n, n + 128)
                value = total[mate, piece, span]
                for k in range(1, size):
                    value = value + arrived[k - 1, r, :, span].astype(jnp.float32)
                value = value + extra_in[r, :, span].astype(jnp.float32)
                final[r, :, span] = (value * scale_cols[piece, :]).astype(jnp.bfloat16)

            @pl.when(s != mate)
            def _():
                along_copy(r).start()

            @pl.when(s == mate)
            def _():
                passing[r] = final[r]

    def deliver():
        @pl.loop(0, parts)
        def _(r):
            @pl.when(s != mate)
            def _():
                along_copy(r).wait_recv()

            @pl.when(s > 0)
            def _():
                across_copy(r).start()

            @pl.when(s == 0)
            def _():
                out_ref[pl.ds(pl.multiple_of(r * some, some), some)] = passing[r]

    def take_up(d, i):
        for j in (2 * i, 2 * i + 1):
            up_landed(d, j).wait_recv()
            if d < last:
                @pl.when((s < last) & (j >= low_up))
                def _():
                    up_copy(d, j).start()

    def take_down(d, i):
        for j in (2 * i, 2 * i + 1):
            down_landed(d, j).wait_recv()
            if d < last:
                @pl.when((s > 0) & (j >= low_down))
                def _():
                    down_copy(d, j).start()

    lower_half = s <= 1
    for d in range(1, size):
        has_down = lower_half & (s + d <= last)
        has_up = (s > 1) & (s - d >= 0)

        @pl.loop(low_here // 2, chunks // 2)
        def _(i):
            if d == 2:
                @pl.when(s == 1)
                def _():
                    take_up(1, i)

                @pl.when(s == last - 1)
                def _():
                    take_down(1, i)

            @pl.when(has_down)
            def _():
                take_down(d, i)

            @pl.when(has_up)
            def _():
                take_up(d, i)

            if d == 2:
                @pl.when(helps)
                def _():
                    multiply(other, 2 * i, low_here, w_ref, total)

            @pl.when(has_down)
            def _():
                multiply(s + d, 2 * i, low_here, w_ref, total)

            @pl.when(has_up)
            def _():
                multiply(s - d, 2 * i, low_here, w_ref, total)

        if d == 2:
            @pl.when(helps)
            def _():
                hand_over(other)

        @pl.when(has_down)
        def _():
            hand_over(s + d)

        @pl.when(has_up)
        def _():
            hand_over(s - d)

        if d == 1:
            @pl.when(helps)
            def _():
                for i in range(gifts):
                    gift_copy(i).wait_recv()
                    swap_copy(i).start()
                for i in range(gifts):
                    swap_landed(i).wait_recv()
                multiply_given(s)
                multiply_given(last - s)

        if d == 2:
            @pl.when(helps)
            def _():
                multiply_given(last - other)

                @pl.when(given_mate != other)
                def _():
                    collect_given()

        @pl.when((apart == d - 1) & (helps | (s == mate)))
        def _():
            collect()

        if d > 1:
            @pl.when((apart == d - 2) & ~with_extra)
            def _():
                deliver()

    @pl.when((apart == last) | with_extra)
    def _():
        collect()

    @pl.when((apart >= last - 1) | with_extra)
    def _():
        deliver()

    @pl.when(at_end)
    def _():
        for i in range(gifts):
            gift_copy(i).wait_send()

    @pl.when(helps)
    def _():
        for i in range(gifts):
            swap_copy(i).wait_send()
        for t in range(size):
            @pl.when((given_mate != t) & (other != t))
            def _():
                @pl.loop(0, parts)
                def _(r):
                    given_copy(t, r).wait_send()

        @pl.when(given_mate != other)
        def _():
            @pl.loop(0, parts)
            def _(r):
                extra_copy(r).wait_send()

    @pl.loop(0, parts)
    def _(r):
        @pl.when(s != mate)
        def _():
            along_copy(r).wait_send()

        @pl.when(s > 0)
        def _():
            across_copy(r).wait()

    @pl.when(s < last)
    def _():
        for each in tail_copies():
            each.wait_send()

        @pl.loop(0, chunks)
        def _(j):
            state_copy(j).wait_send()

    for k in range(1, size):
        sums_copy(k).wait_send()

    for t in range(size):
        @pl.when(mate != t)
        def _():
            @pl.loop(0, parts)
            def _(r):
                partial_copy(t, r).wait_send()

    for d in range(last):
        @pl.when((s < last) & (s - d >= 0))
        def _():
            @pl.loop(low_up, chunks)
            def _(j):
                up_copy(d, j).wait_send()

        @pl.when((s > 0) & (s + d <= last))
        def _():
            @pl.loop(low_down, chunks)
            def _(j):
                down_copy(d, j).wait_send()


def square_shards(
    x_in, bc_in, z_in, dt_raw, dt_bias, a_log, d_skip, conv_x, conv_bc, norm_gain, out_weight
):
    size = lax.axis_size("seq")
    height, width = x_in.shape
    heads = dt_raw.shape[1]
    groups = bc_in.shape[1] // (2 * N)
    chunks = heads // CHUNK_HEADS
    wide = CHUNK_HEADS * P_SIZE
    columns = out_weight.shape[1]
    parts = 4
    given = chunks // 2
    gifts = 4
    some = height // parts
    narrow = jnp.bfloat16
    dma = pltpu.SemaphoreType.DMA
    operands = (
        x_in, bc_in, z_in, dt_raw, dt_bias[None, :], a_log[None, :], d_skip[None, :],
        conv_x, conv_bc, norm_gain[None, :], out_weight,
    )
    return pl.pallas_call(
        lambda *refs: layer_kernel(size, H * P_SIZE, *refs),
        out_shape=jax.ShapeDtypeStruct((height, columns), narrow),
        in_specs=[pl.BlockSpec(memory_space=pltpu.VMEM)] * len(operands),
        out_specs=pl.BlockSpec(memory_space=pltpu.VMEM),
        scratch_shapes=[
            pltpu.VMEM((TAIL, width), narrow),
            pltpu.VMEM((TAIL, groups * 2 * N), narrow),
            pltpu.VMEM((TAIL + height, wide), jnp.float32),
            pltpu.VMEM((chunks, height, 4 * heads), jnp.float32),
            pltpu.VMEM((chunks, 2 * CHUNK_HEADS, height), jnp.float32),
            pltpu.VMEM((groups, height, height), jnp.float32),
            pltpu.VMEM((groups, N, height), narrow),
            pltpu.VMEM((groups, height, N), narrow),
            pltpu.VMEM((chunks, N, wide), narrow),
            pltpu.VMEM((chunks, N, wide), narrow),
            pltpu.VMEM((8, height), jnp.float32),
            pltpu.VMEM((size - 1, 8, height), jnp.float32),
            pltpu.VMEM((8, height), jnp.float32),
            pltpu.VMEM((8, height), jnp.float32),
            pltpu.VMEM((size, chunks, height, wide), narrow),
            pltpu.VMEM((size, height, columns), jnp.float32),
            pltpu.VMEM((size, parts, some, columns), narrow),
            pltpu.VMEM((size - 1, parts, some, columns), narrow),
            pltpu.VMEM((parts, some, columns), narrow),
            pltpu.VMEM((parts, some, columns), narrow),
            pltpu.VMEM((height, 128), jnp.float32),
            pltpu.VMEM((given * wide, columns), narrow),
            pltpu.VMEM((size, height, columns), jnp.float32),
            pltpu.VMEM((size, parts, some, columns), narrow),
            pltpu.VMEM((size - 1, parts, some, columns), narrow),
            pltpu.VMEM((parts, some, columns), narrow),
            pltpu.VMEM((parts, some, columns), narrow),
            dma((2,)), dma((2,)),
            dma((chunks,)), dma((chunks,)),
            dma((size - 1,)), dma((size - 1,)),
            dma, dma,
            dma((size - 1, chunks)), dma((size - 1, chunks)),
            dma((size - 1, chunks)), dma((size - 1, chunks)),
            dma((size, parts)), dma((size - 1, parts)),
            dma((parts,)), dma((parts,)),
            dma((parts,)), dma((parts,)),
            dma((gifts,)), dma((gifts,)),
            dma((gifts,)), dma((gifts,)),
            dma((size, parts)), dma((size - 1, parts)),
            dma((parts,)), dma((parts,)),
        ],
        compiler_params=pltpu.CompilerParams(
            collective_id=0, has_side_effects=True, vmem_limit_bytes=52 * 1024 * 1024
        ),
        cost_estimate=pl.CostEstimate(
            flops=2 * size * height * width * columns, bytes_accessed=9 * height * width,
            transcendentals=heads * height * height,
        ),
        name="layer",
    )(*operands)


def from_behind(block, axis, distance):
    devices = range(lax.axis_size(axis))
    route = [(i - distance, i) for i in devices if i - distance in devices]
    return lax.ppermute(block, axis, route)


def conv_with(before, current, weight):
    height = current.shape[0]
    joined = jnp.concatenate([before, current], axis=0).astype(jnp.float32)
    summed = jnp.zeros(current.shape, jnp.float32)
    for offset in range(CONV):
        summed = summed + weight[offset][None, :] * joined[offset : offset + height]
    return summed


def shards(
    x_in, bc_in, z_in, dt_raw, dt_bias, a_log, d_skip, conv_x, conv_bc, norm_gain, out_weight
):
    height = x_in.shape[0]
    heads = dt_raw.shape[1]
    local_width = x_in.shape[1]
    nearby_groups = bc_in.shape[1] // (2 * N)
    per_group = heads // nearby_groups
    tails = from_behind((x_in[height - (CONV - 1) :], bc_in[height - (CONV - 1) :]), "seq", 1)
    input_convolved = jax.nn.silu(conv_with(tails[0], x_in, conv_x)).astype(jnp.bfloat16)
    bc_conv = jax.nn.silu(conv_with(tails[1], bc_in, conv_bc)).astype(jnp.bfloat16)
    step_sizes = jax.nn.softplus(dt_raw + dt_bias[None, :])
    log_decay = -jnp.exp(a_log)[None, :] * step_sizes
    blocks = height // BLOCK
    x_blocks = input_convolved.reshape(blocks, BLOCK, heads, P_SIZE)
    bc_blocks = bc_conv.reshape(blocks, BLOCK, nearby_groups, 2, N)
    b_mat = bc_blocks[:, :, :, 0]
    c_mat = bc_blocks[:, :, :, 1]
    running = jnp.cumsum(log_decay.reshape(blocks, BLOCK, heads), axis=1)
    step_blocks = step_sizes.reshape(blocks, BLOCK, heads)
    places = jnp.arange(BLOCK, dtype=jnp.int32)
    lower = places[:, None] >= places[None, :]

    def inside(input_rows):
        x_here, b_here, c_here, run_here, step_here = input_rows
        scores = jnp.einsum("ign,jgn->gij", c_here, b_here, preferred_element_type=jnp.float32)
        run_heads = run_here.T.reshape(nearby_groups, per_group, BLOCK)
        step_heads = step_here.T.reshape(nearby_groups, per_group, BLOCK)
        spread = run_heads[:, :, :, None] - run_heads[:, :, None, :]
        spread = jnp.where(lower[None, None], spread, -jnp.inf)
        mixing = (scores[:, None] * jnp.exp(spread) * step_heads[:, :, None, :]).astype(
            jnp.bfloat16
        )
        mixing = mixing.reshape(heads, BLOCK, BLOCK)
        within = jnp.einsum("hij,jhp->ihp", mixing, x_here, preferred_element_type=jnp.float32)
        until_finish = jnp.exp(run_here[-1:] - run_here) * step_here
        b_heads = jnp.repeat(b_here.astype(jnp.float32), per_group, axis=1)
        weighted_b = (b_heads * until_finish[:, :, None]).astype(jnp.bfloat16)
        fresh = jnp.einsum("jhn,jhp->hnp", weighted_b, x_here, preferred_element_type=jnp.float32)
        return (within, fresh)

    within, fresh = lax.map(inside, (x_blocks, b_mat, c_mat, running, step_blocks))
    since_beginning = (
        jnp.repeat(c_mat.astype(jnp.float32), per_group, axis=2) * jnp.exp(running)[..., None]
    )
    block_decay = running[:, -1, :]
    state = jnp.zeros((heads, N, P_SIZE), jnp.float32)
    prefix = jnp.zeros((heads,), jnp.float32)
    starts = [state]
    offsets = [prefix]
    state = jnp.exp(block_decay[0])[:, None, None] * state + fresh[0]
    prefix = block_decay[0]
    start_states = jnp.stack(starts)
    start_logs = jnp.stack(offsets)
    totals = lax.all_gather(prefix[None, :], "seq", axis=0, tiled=True)
    ends = jnp.cumsum(totals, axis=0)
    before = jnp.concatenate([jnp.zeros((1, heads), jnp.float32), ends[:-1]], axis=0)
    own_index = lax.axis_index("seq")
    own_before = lax.dynamic_index_in_dim(before, own_index, 0, keepdims=False)
    piece = lax.all_gather(state[None], "seq", axis=0, tiled=True)
    quantity = piece.shape[0]
    reference_point = jnp.arange(quantity, dtype=jnp.int32)
    exponent = jnp.where(
        (reference_point < own_index)[:, None], own_before[None, :] - ends, -jnp.inf
    )
    incoming = jnp.einsum("kh,khnp->hnp", jnp.exp(exponent), piece, precision=lax.Precision.HIGHEST)
    full_starts = start_states + jnp.exp(start_logs)[:, :, None, None] * incoming[None]
    across = jnp.einsum(
        "cihn,chnp->cihp", since_beginning, full_starts, precision=lax.Precision.HIGHEST
    )
    mixed = within + across + d_skip[None, None, :, None] * x_blocks.astype(jnp.float32)
    mixed = mixed.reshape(height, local_width)
    gated = mixed * jax.nn.silu(z_in.astype(jnp.float32))
    square_sums = lax.psum(jnp.sum(gated * gated, axis=1), "head")
    normed = (
        gated * lax.rsqrt(square_sums / (H * P_SIZE) + epsilon)[:, None] * norm_gain[None, :]
    ).astype(jnp.bfloat16)
    terms = jnp.dot(
        normed,
        lax.all_gather(out_weight, "seq", axis=1, tiled=True),
        preferred_element_type=jnp.float32,
    )
    return lax.psum_scatter(terms, "head", scatter_dimension=1, tiled=True).astype(jnp.bfloat16)


def solution(mesh):
    placed = (
        P(("dp", "seq"), "head"),
        P(("dp", "seq"), "head"),
        P(("dp", "seq"), "head"),
        P(("dp", "seq"), "head"),
        P("head"),
        P("head"),
        P("head"),
        P(None, "head"),
        P(None, "head"),
        P("head"),
        P("head", "seq"),
    )
    shape = mesh.shape
    square = shape["seq"] == 4 and shape["head"] == 4 and shape["dp"] == 2
    return jax.shard_map(
        square_shards if square else shards, mesh=mesh, in_specs=placed, out_specs=P(("dp", "seq"), "head"), check_vma=False
    )
```
